512 devices in a mesh: dp: 8 (over x, core), expouter: 8 (over z_lo), expinner: 8 (over z_hi, y).
Axes of the slice: x: 4, y: 4, z: 16 (z_hi: 2, z_lo: 8; z = z_hi * 8 + z_lo), core: 2. Of those that a mesh axis runs over, the one named last changes fastest.
Arguments:
- tokens: bfloat16 [65536, 1024], P(('dp', 'expouter', 'expinner')), may hold values from -6 to 6
- cotangent: bfloat16 [65536, 1024], P(('dp', 'expouter', 'expinner')), may hold values from -6 to 6
- gate_probs: float32 [65536, 2], P(('dp', 'expouter', 'expinner')), may hold values from 0.05 to 1
- expert_ids: int32 [65536, 2], P(('dp', 'expouter', 'expinner')), may hold values from 0 to 63, all different within a row; in each aligned block of 128 rows (0 to 127, 128 to 255, ...) at most 5 rows name the same one
- gate_weight: bfloat16 [64, 1024, 768], P(('expouter', 'expinner'), 'dp'), may hold values from -0.1875 to 0.1875
- up_weight: bfloat16 [64, 1024, 768], P(('expouter', 'expinner'), 'dp'), may hold values from -0.1875 to 0.1875
- down_weight: bfloat16 [64, 1024, 768], P(('expouter', 'expinner'), 'dp'), may hold values from -0.21875 to 0.21875
Outputs:
- mixed: bfloat16 [65536, 1024], P(('dp', 'expouter', 'expinner'))
- grad_tokens: bfloat16 [65536, 1024], P(('dp', 'expouter', 'expinner'))
- grad_probs: float32 [65536, 2], P(('dp', 'expouter', 'expinner'))
- grad_gate: float32 [64, 1024, 768], P(('expouter', 'expinner'), 'dp')
- grad_up: float32 [64, 1024, 768], P(('expouter', 'expinner'), 'dp')
- grad_down: float32 [64, 1024, 768], P(('expouter', 'expinner'), 'dp')
The draws below stay inside these ranges and needn't reach their ends.
Inputs may be any that keep to these rules, and one draw needn't show every extreme that they name: `expert_ids`: among the tokens of one device (aligned blocks of 128 tokens) no expert is named more than 5 times, a bound that some block reaches; a token's 2 experts differ.
All inputs are finite; a program needn't handle non-finite values.
Results may differ from the reference program's by a relative error of at most 0.0065.
Values may be sent and summed in bfloat16 or wider, within the bound.
A program may use at most 64 MiB of HBM per device.

```python
import math
import jax
import jax.numpy as jnp
import numpy as np
from jax import lax

D = 1024
H = 768
TOP = 2
TOK_DEV = 128
EXPERTS = 64
CAP = 5
TOKENS = 65536


def steps_of(key, extent, shards, smallest, high):
    def one(dim, parts):
        draws = jax.random.uniform(jax.random.fold_in(jax.random.fold_in(key, 6), dim), (parts,), jnp.float32, smallest / len(shards), high / len(shards))
        return jnp.repeat(jnp.exp(draws), extent[dim] // parts).reshape((-1,) + (1,) * (len(extent) - dim - 1))

    loudness = one(*shards[0])
    for cut in shards[1:]:
        loudness = loudness * one(*cut)
    return loudness


def assign_block(stream_key, own, number, rows, amount, top, most, lean):
    order = jax.random.permutation(stream_key, amount)
    crowded, common = shares(amount, rows * top, most, lean, True), shares(amount, rows * top, most, lean, False)
    places = jnp.arange(amount)

    def named(lengths, rotation):
        used = int((lengths > 0).sum())
        fixed = max(1, used // 4)
        passed = fixed + (places - fixed + rotation * (used - fixed)) % max(1, amount - fixed)
        return jnp.zeros((amount,), jnp.int32).at[order[jnp.where(places < fixed, places, passed)]].set(jnp.asarray(lengths, jnp.int32))

    lengths = jnp.where(number % 4 == 0, named(crowded, number // 4), named(common, number - number // 4 - 1))
    mixed = jax.random.permutation(jax.random.fold_in(own, 3), amount)
    source_of, taker = mixed[0:amount // 2 * 2:2], mixed[1:amount // 2 * 2:2]
    slack = jnp.minimum(lengths[source_of] - 1, most - lengths[taker]) // 2
    slack = jnp.where((source_of == order[0]) | (taker == order[0]) | (lengths[taker] == 0), 0, jnp.maximum(slack, 0))
    passed = jax.random.randint(jax.random.fold_in(own, 4), (amount // 2,), 0, 1 << 20) % (slack + 1)
    lengths = lengths.at[source_of].add(-passed).at[taker].add(passed)
    labels = jnp.searchsorted(jnp.cumsum(lengths), jnp.arange(rows * top), side="right").astype(jnp.int32)
    table = labels.reshape(top, rows).T
    table = table[jax.random.permutation(jax.random.fold_in(own, 1), rows)]
    rotation = jax.random.randint(jax.random.fold_in(own, 2), (rows, 1), 0, top)
    return jnp.take_along_axis(table, (jnp.arange(top)[None, :] + rotation) % top, axis=1)


def shares(count, total, limit, skew, full):
    loads = [(1 << 20) // math.isqrt(standing ** skew) + 1 for standing in range(1, count + 1)]
    largest = limit if full else min(limit, max(-(-total // count), total * loads[0] // sum(loads)))
    least = 1 if total - largest >= count - 1 else 0
    holding, spare = [largest] + [least] * (count - 1), total - largest - least * (count - 1)
    while spare > 0:
        candidates = [i for i in range(1, count) if holding[i] < largest] or [i for i in range(1, count) if holding[i] < limit]
        whole, left = sum([loads[i] for i in candidates]), spare
        for i in candidates:
            extra = min(limit - holding[i], max(1, left * loads[i] // whole), spare)
            holding[i] = holding[i] + extra
            spare = spare - extra
    return np.array(holding)


def gaussian(rng, extent, scale, most, pieces=(), kind=jnp.bfloat16):
    array = scale * jax.random.normal(rng, extent, jnp.float32)
    if pieces:
        array = array * steps_of(rng, extent, pieces, -0.22, 0.18)
    return jnp.clip(array, -most, most).astype(kind)


def setup_inputs(seed: int = 0) -> dict:
    seeds = jax.random.split(jax.random.key(seed), 8)
    tokens = gaussian(seeds[0], (TOKENS, D), 1.0, 6.0, ((0, 512),))
    cotangent = gaussian(seeds[1], (TOKENS, D), 1.0, 6.0, ((0, 512),))
    gate_probs = jnp.clip(jnp.exp(math.log(1.0) - 2.9957323 * jax.random.uniform(seeds[2], (TOKENS, TOP), jnp.float32) ** steps_of(seeds[2], (TOKENS, TOP), ((0, 512),), -0.2, 0.2)), 0.05, 1.0)
    expert_ids_keys = jax.random.split(jax.random.fold_in(seeds[3], 1), TOKENS // TOK_DEV)
    expert_ids_turns = jax.random.permutation(jax.random.fold_in(seeds[3], 3), TOKENS // TOK_DEV)
    expert_ids = jax.vmap(lambda own, number: assign_block(jax.random.fold_in(seeds[3], 2), own, number, TOK_DEV, EXPERTS, TOP, CAP, 2))(expert_ids_keys, expert_ids_turns).reshape((TOKENS, TOP))
    gate_weight = gaussian(seeds[4], (EXPERTS, D, H), D ** -0.5, 0.1875, ((0, 64), (1, 8)))
    up_weight = gaussian(seeds[5], (EXPERTS, D, H), D ** -0.5, 0.1875, ((0, 64), (1, 8)))
    down_weight = gaussian(seeds[6], (EXPERTS, D, H), H ** -0.5, 0.21875, ((0, 64), (1, 8)))
    return dict(tokens=tokens, cotangent=cotangent, gate_probs=gate_probs, expert_ids=expert_ids, gate_weight=gate_weight, up_weight=up_weight, down_weight=down_weight)


def expert_pass(rows_x, rows_o, gate_mat, up_mat, down_mat):
    pre_gate = jnp.dot(rows_x, gate_mat, preferred_element_type=jnp.float32)
    pre_up = jnp.dot(rows_x, up_mat, preferred_element_type=jnp.float32)
    sigma = jax.nn.sigmoid(pre_gate)
    active = pre_gate * sigma
    hidden = (active * pre_up).astype(jnp.bfloat16)
    expert_out = jnp.dot(hidden, down_mat.T, preferred_element_type=jnp.float32).astype(jnp.bfloat16)
    grad_hidden = jnp.dot(rows_o, down_mat, preferred_element_type=jnp.float32)
    slope = sigma * (1.0 + pre_gate * (1.0 - sigma))
    grad_gate_pre = (grad_hidden * pre_up * slope).astype(jnp.bfloat16)
    grad_up_pre = (grad_hidden * active).astype(jnp.bfloat16)
    grad_rows = (jnp.dot(grad_gate_pre, gate_mat.T, preferred_element_type=jnp.float32)
                 + jnp.dot(grad_up_pre, up_mat.T, preferred_element_type=jnp.float32)).astype(jnp.bfloat16)
    return hidden, expert_out, grad_gate_pre, grad_up_pre, grad_rows


def reference(tokens, cotangent, gate_probs, expert_ids, gate_weight, up_weight, down_weight):
    blocks = TOKENS // TOK_DEV
    assigns = TOK_DEV * TOP
    slots_all = EXPERTS * CAP
    flat_route = expert_ids.reshape(blocks, assigns)
    onehot = (flat_route[:, :, None] == jnp.arange(EXPERTS, dtype=jnp.int32)[None, None, :]).astype(jnp.int32)
    earlier = jnp.cumsum(onehot, axis=1) - onehot
    slot_pos = jnp.sum(earlier * onehot, axis=2).astype(jnp.int32)
    target = (flat_route * CAP + slot_pos).astype(jnp.int32)
    block_ids = jnp.arange(blocks, dtype=jnp.int32)[:, None]
    source = jnp.full((blocks, slots_all), assigns, jnp.int32)
    source = source.at[block_ids, target].set(jnp.arange(assigns, dtype=jnp.int32)[None, :])
    padding = jnp.zeros((blocks, 1, D), jnp.bfloat16)
    token_rows = jnp.repeat(tokens.reshape(blocks, TOK_DEV, D), TOP, axis=1)
    token_rows = jnp.concatenate([token_rows, padding], axis=1)
    scaled = (gate_probs.reshape(blocks, TOK_DEV, TOP, 1)
              * cotangent.reshape(blocks, TOK_DEV, 1, D).astype(jnp.float32)).astype(jnp.bfloat16)
    scaled = jnp.concatenate([scaled.reshape(blocks, assigns, D), padding], axis=1)

    def per_expert(index):
        columns = lax.dynamic_slice_in_dim(source, (index * CAP).astype(jnp.int32), CAP, 1)
        rows_x = token_rows[block_ids, columns].reshape(blocks * CAP, D)
        rows_o = scaled[block_ids, columns].reshape(blocks * CAP, D)
        hidden, expert_out, grad_gate_pre, grad_up_pre, grad_rows = expert_pass(
            rows_x, rows_o, gate_weight[index], up_weight[index], down_weight[index])
        grad_g = jnp.dot(rows_x.T, grad_gate_pre, preferred_element_type=jnp.float32)
        grad_u = jnp.dot(rows_x.T, grad_up_pre, preferred_element_type=jnp.float32)
        grad_d = jnp.dot(rows_o.T, hidden, preferred_element_type=jnp.float32)
        return (expert_out.reshape(blocks, CAP, D), grad_rows.reshape(blocks, CAP, D), grad_g, grad_u, grad_d)

    outs_all, rows_all, grad_gate, grad_up, grad_down = lax.map(per_expert, jnp.arange(EXPERTS, dtype=jnp.int32))
    pick_out = outs_all[flat_route, block_ids, slot_pos].reshape(blocks, TOK_DEV, TOP, D).astype(jnp.float32)
    pick_grad = rows_all[flat_route, block_ids, slot_pos].reshape(blocks, TOK_DEV, TOP, D).astype(jnp.float32)
    mixed = jnp.sum(gate_probs.reshape(blocks, TOK_DEV, TOP, 1) * pick_out, axis=2).astype(jnp.bfloat16)
    grad_tokens = jnp.sum(pick_grad, axis=2).astype(jnp.bfloat16)
    grad_probs = jnp.sum(cotangent.reshape(blocks, TOK_DEV, 1, D).astype(jnp.float32) * pick_out, axis=3)
    return (mixed.reshape(TOKENS, D), grad_tokens.reshape(TOKENS, D), grad_probs.reshape(TOKENS, TOP),
            grad_gate, grad_up, grad_down)
```

```python
import jax
import jax.numpy as jnp
from jax import lax
from jax.sharding import PartitionSpec as P


def expert_pass(rows_x, rows_o, gate_mat, up_mat, down_mat):
    pre_gate = jnp.dot(rows_x, gate_mat, preferred_element_type=jnp.float32)
    pre_up = jnp.dot(rows_x, up_mat, preferred_element_type=jnp.float32)
    sigma = jax.nn.sigmoid(pre_gate)
    active = pre_gate * sigma
    hidden = (active * pre_up).astype(jnp.bfloat16)
    expert_out = jnp.dot(hidden, down_mat.T, preferred_element_type=jnp.float32).astype(
        jnp.bfloat16
    )
    grad_hidden = jnp.dot(rows_o, down_mat, preferred_element_type=jnp.float32)
    slope = sigma * (1.0 + pre_gate * (1.0 - sigma))
    grad_gate_pre = (grad_hidden * pre_up * slope).astype(jnp.bfloat16)
    grad_up_pre = (grad_hidden * active).astype(jnp.bfloat16)
    grad_rows = (
        jnp.dot(grad_gate_pre, gate_mat.T, preferred_element_type=jnp.float32)
        + jnp.dot(grad_up_pre, up_mat.T, preferred_element_type=jnp.float32)
    ).astype(jnp.bfloat16)
    return (hidden, expert_out, grad_gate_pre, grad_up_pre, grad_rows)


def contract_rows(left, right):
    return lax.dot_general(
        left, right, (((0,), (0,)), ((), ())), preferred_element_type=jnp.float32
    )


def per_device(tokens, cotangent, gate_probs, expert_ids, gate_weight, up_weight, down_weight):
    tok_rows, model_width = tokens.shape
    top_count = expert_ids.shape[1]
    outer_count = lax.axis_size("expouter")
    inner_count = lax.axis_size("expinner")
    expert_count = outer_count * inner_count
    capacity = max(2, tok_rows * top_count * 5 // (4 * expert_count))
    slots_all = expert_count * capacity
    assigns = tok_rows * top_count
    flat_route = expert_ids.reshape(assigns)
    order = jnp.arange(assigns, dtype=jnp.int32)
    before = (order[None, :] < order[:, None]) & (flat_route[None, :] == flat_route[:, None])
    slot_pos = jnp.sum(before.astype(jnp.int32), axis=1)
    target = flat_route * capacity + slot_pos
    select = (target[None, :] == jnp.arange(slots_all, dtype=jnp.int32)[:, None]).astype(
        jnp.bfloat16
    )
    token_select = select.reshape(slots_all, tok_rows, top_count).sum(axis=2)
    send_x = jnp.dot(token_select, tokens, preferred_element_type=jnp.float32).astype(jnp.bfloat16)
    scaled = (gate_probs[:, :, None] * cotangent[:, None, :].astype(jnp.float32)).astype(
        jnp.bfloat16
    )
    send_o = jnp.dot(
        select, scaled.reshape(assigns, model_width), preferred_element_type=jnp.float32
    ).astype(jnp.bfloat16)
    weights_all = (
        lax.all_gather(gate_weight, "dp", axis=1, tiled=True),
        lax.all_gather(up_weight, "dp", axis=1, tiled=True),
        lax.all_gather(down_weight, "dp", axis=1, tiled=True),
    )
    gate_full = weights_all[0][0]
    up_full = weights_all[1][0]
    down_full = weights_all[2][0]
    shaped = (
        send_x.reshape(expert_count, capacity, model_width),
        send_o.reshape(expert_count, capacity, model_width),
    )
    recv_x, recv_o = (
        lax.all_to_all(
            shaped[0], ("expouter", "expinner"), split_axis=0, concat_axis=0, tiled=True
        ),
        lax.all_to_all(
            shaped[1], ("expouter", "expinner"), split_axis=0, concat_axis=0, tiled=True
        ),
    )
    rows_x = recv_x.reshape(slots_all, model_width)
    rows_o = recv_o.reshape(slots_all, model_width)
    hidden, expert_out, grad_gate_pre, grad_up_pre, grad_rows = expert_pass(
        rows_x, rows_o, gate_full, up_full, down_full
    )
    returned = (
        expert_out.reshape(expert_count, capacity, model_width),
        grad_rows.reshape(expert_count, capacity, model_width),
    )
    back_out, back_grad = (
        lax.all_to_all(
            returned[0], ("expouter", "expinner"), split_axis=0, concat_axis=0, tiled=True
        ),
        lax.all_to_all(
            returned[1], ("expouter", "expinner"), split_axis=0, concat_axis=0, tiled=True
        ),
    )
    pick_out = back_out.reshape(slots_all, model_width)[target].reshape(
        tok_rows, top_count, model_width
    )
    pick_grad = back_grad.reshape(slots_all, model_width)[target].reshape(
        tok_rows, top_count, model_width
    )
    pick_float = pick_out.astype(jnp.float32)
    mixed = jnp.sum(gate_probs[:, :, None] * pick_float, axis=1).astype(jnp.bfloat16)
    grad_tokens = jnp.sum(pick_grad.astype(jnp.float32), axis=1).astype(jnp.bfloat16)
    grad_probs = jnp.sum(cotangent[:, None, :].astype(jnp.float32) * pick_float, axis=2)
    cols_x, cols_o = (
        lax.all_to_all(rows_x, "dp", split_axis=1, concat_axis=0, tiled=True),
        lax.all_to_all(rows_o, "dp", split_axis=1, concat_axis=0, tiled=True),
    )
    grad_g = contract_rows(cols_x, lax.all_gather(grad_gate_pre, "dp", axis=0, tiled=True))
    grad_u = contract_rows(cols_x, lax.all_gather(grad_up_pre, "dp", axis=0, tiled=True))
    grad_d = contract_rows(cols_o, lax.all_gather(hidden, "dp", axis=0, tiled=True))
    return (mixed, grad_tokens, grad_probs, grad_g[None], grad_u[None], grad_d[None])


def solution(mesh):
    return jax.shard_map(
        per_device,
        mesh=mesh,
        in_specs=(
            P(("dp", "expouter", "expinner"), None),
            P(("dp", "expouter", "expinner"), None),
            P(("dp", "expouter", "expinner"), None),
            P(("dp", "expouter", "expinner"), None),
            P(("expouter", "expinner"), "dp", None),
            P(("expouter", "expinner"), "dp", None),
            P(("expouter", "expinner"), "dp", None),
        ),
        out_specs=(
            P(("dp", "expouter", "expinner"), None),
            P(("dp", "expouter", "expinner"), None),
            P(("dp", "expouter", "expinner"), None),
            P(("expouter", "expinner"), "dp", None),
            P(("expouter", "expinner"), "dp", None),
            P(("expouter", "expinner"), "dp", None),
        ),
        check_vma=False,
    )
```

```python
import functools

import jax
import jax.numpy as jnp
from jax import lax
from jax.experimental import pallas as pl
from jax.experimental.pallas import tpu as pltpu
from jax.sharding import PartitionSpec as P

MESH = pl.DeviceIdType.MESH
F32 = jnp.float32
BF16 = jnp.bfloat16
LANES = 128
NY = 4
CAP = 5


def fifth(v):
    return (v * 52429) >> 18


def kernel(
    nx, nz_lo, nz_hi, ny,
    tok, cot, probs, ids, wg, wu, wd,
    mixed, gtok, gprob, og, ou, od,
    weights, send, recv, rsend, rrecv, wide, xo, acts, scaled,
    csend, crecv, xsend, xrecv, acc, back,
    load_sem, fs_sem, fr_sem, rs_sem, rr_sem,
    wxs_sem, wxr_sem, wcs_sem, wcr_sem,
    gcs_sem, gcr_sem, gxs_sem, gxr_sem,
):
    nz = nz_lo * nz_hi
    width = tok.shape[1]
    chunks = width // LANES
    tall = 2 * chunks
    group = nz * CAP
    hidden_n = wg.shape[2]
    me = lax.axis_index("dp")
    x, core = me // 2, me % 2
    inner = lax.axis_index("expinner")
    y = inner % ny
    z = (inner // ny) * nz_lo + lax.axis_index("expouter")

    def at_yz(dy, dz):
        tz = lax.rem(z + dz + nz, nz)
        ty = lax.rem(y + dy + ny, ny)
        return {"expouter": lax.rem(tz, nz_lo), "expinner": (tz // nz_lo) * ny + ty}

    def at_x(dx):
        return {"dp": lax.rem(x + dx, nx) * 2 + core}

    twin = {"dp": x * 2 + 1 - core}

    def remote(src, dst, ss, rs, device):
        return pltpu.make_async_remote_copy(
            src_ref=src, dst_ref=dst, send_sem=ss, recv_sem=rs,
            device_id=device, device_id_type=MESH,
        )

    own = [pltpu.make_async_copy(w.at[0], weights.at[m, me], load_sem.at[m]) for m, w in enumerate((wg, wu, wd))]
    for copy in own:
        copy.start()
    barrier = pltpu.get_barrier_semaphore()

    def greet(i, _):
        pl.semaphore_signal(barrier, inc=1, device_id=at_yz(i // nz, lax.rem(i, nz)), device_id_type=MESH)
        return 0

    lax.fori_loop(1, ny * nz, greet, 0)
    for dx in range(1, nx):
        pl.semaphore_signal(barrier, inc=1, device_id=at_x(dx), device_id_type=MESH)
    pl.semaphore_signal(barrier, inc=1, device_id=twin, device_id_type=MESH)

    rows = tok.shape[0]
    idf = ids[...].astype(F32)
    down_id = [jnp.broadcast_to(idf[:, k:k + 1], (rows, rows)) for k in range(2)]
    over_id = [jnp.transpose(b) for b in down_id]
    first = lax.broadcasted_iota(jnp.int32, (rows, rows), 0)
    second = lax.broadcasted_iota(jnp.int32, (rows, rows), 1)
    col_target, row_target = [], []
    for k in range(2):
        hits = sum(jnp.where((down_id[k] == over_id[j]) & (second < first), 1.0, 0.0) for j in range(2))
        col_target.append(idf[:, k:k + 1] * CAP + jnp.sum(hits, axis=1, keepdims=True))
        hits = sum(jnp.where((down_id[j] == over_id[k]) & (first < second), 1.0, 0.0) for j in range(2))
        row_target.append(over_id[k][0:1, :] * CAP + jnp.sum(hits, axis=0, keepdims=True))
    pr = [probs[:, k:k + 1] for k in range(2)]
    for k in range(2):
        scaled[k * rows:(k + 1) * rows, :] = (pr[k] * cot[...].astype(F32)).astype(BF16)

    def slot_id(dy, q, slot):
        tz = (z + q) & (nz - 1)
        ty = (y + dy) & (ny - 1)
        expert = (tz & (nz_lo - 1)) * (nz_hi * ny) + (tz // nz_lo) * ny + ty
        return (expert * CAP + slot).astype(F32)

    line = lax.broadcasted_iota(jnp.int32, (group, 1), 0)
    line_dz = fifth(line)
    line_slot = line - CAP * line_dz

    def pack(dy):
        wanted = slot_id(dy, line_dz, line_slot)
        sel = [jnp.where(wanted == row_target[k], 1.0, 0.0) for k in range(2)]
        both = (sel[0] + sel[1]).astype(BF16)
        each = jnp.concatenate(sel, axis=1).astype(BF16)
        rows_x = jnp.dot(both, tok[...], preferred_element_type=F32)
        rows_o = jnp.dot(each, scaled[...], preferred_element_type=F32)
        for c in range(chunks):
            cols = slice(c * LANES, (c + 1) * LANES)
            wide[pl.ds(c, group, stride=tall), :] = rows_x[:, cols]
            wide[pl.ds(chunks + c, group, stride=tall), :] = rows_o[:, cols]
        send[pl.ds(dy * nz, nz)] = wide[...].astype(BF16).reshape(nz, CAP * tall, LANES)

    def scatter(dy, src, dst, ss, rs, sign):
        def one(dz, _):
            i = dy * nz + dz

            @pl.when(i > 0)
            def _():
                remote(src.at[i], dst.at[i], ss, rs.at[dy], at_yz(sign * dy, sign * dz)).start()

            return 0

        lax.fori_loop(0, nz, one, 0)

        @pl.when(dy == 0)
        def _():
            pltpu.make_async_copy(src.at[0], dst.at[0], rs.at[0]).start()

    pack(jnp.int32(0))
    for copy in own:
        copy.wait()
    pl.semaphore_wait(barrier, ny * nz - 1 + nx - 1 + 1)

    mine = weights.at[:, me]
    remote(mine, mine, wcs_sem.at[0], wcr_sem.at[0], twin).start()
    for dx in range(1, nx):
        remote(mine, mine, wxs_sem.at[dx], wxr_sem.at[dx], at_x(dx)).start()

    scatter(jnp.int32(0), send, recv, fs_sem, fr_sem, 1)

    def pack_and_send(dy, _):
        pack(dy)
        scatter(dy, send, recv, fs_sem, fr_sem, 1)
        return 0

    lax.fori_loop(1, ny, pack_and_send, 0)

    for dx in range(1, nx):
        theirs = weights.at[:, lax.rem(x - dx + nx, nx) * 2 + core]
        remote(theirs, theirs, wxs_sem.at[dx], wxr_sem.at[dx], at_x(dx)).wait_recv()
        remote(theirs, theirs, wcs_sem.at[dx], wcr_sem.at[dx], twin).start()
    for dx in range(nx):
        theirs = weights.at[:, lax.rem(x - dx + nx, nx) * 2 + 1 - core]
        remote(theirs, theirs, wcs_sem.at[dx], wcr_sem.at[dx], twin).wait_recv()

    def unpack(buf, dy, out):
        wide[...] = buf[pl.ds(dy * nz, nz)].reshape(nz * CAP * tall, LANES).astype(F32)
        here = pl.ds(pl.multiple_of(dy * group, 16), group)
        for part in range(2):
            for c in range(chunks):
                out[part, c, here, :] = wide[pl.ds(part * chunks + c, group, stride=tall), :].astype(BF16)

    step = 256

    def expert(dy, _):
        remote(
            recv.at[pl.ds(dy * nz, nz)], recv.at[pl.ds(dy * nz, nz)], fs_sem, fr_sem.at[dy], twin
        ).wait_recv()
        unpack(recv, dy, xo)
        here = pl.ds(pl.multiple_of(dy * group, 16), group)
        rows_x = jnp.concatenate([xo[0, c, here, :] for c in range(chunks)], axis=1)
        rows_o = jnp.concatenate([xo[1, c, here, :] for c in range(chunks)], axis=1)

        def up(n, _):
            cols = pl.ds(pl.multiple_of(n * step, step), step)
            gate = jnp.dot(rows_x, weights[0, :, :, cols].reshape(width, step), preferred_element_type=F32)
            lift = jnp.dot(rows_x, weights[1, :, :, cols].reshape(width, step), preferred_element_type=F32)
            grad = jnp.dot(rows_o, weights[2, :, :, cols].reshape(width, step), preferred_element_type=F32)
            sigma = jax.nn.sigmoid(gate)
            active = gate * sigma
            slope = sigma * (1.0 + gate * (1.0 - sigma))
            acts[0, here, cols] = (grad * lift * slope).astype(BF16)
            acts[1, here, cols] = (grad * active).astype(BF16)
            acts[2, here, cols] = (active * lift).astype(BF16)
            return 0

        lax.fori_loop(0, hidden_n // step, up, 0)

        def turned(a, m, d):
            w = weights[m, pl.ds(d * 2, 2)].reshape(2 * LANES, hidden_n)
            return lax.dot_general(a, w, (((1,), (1,)), ((), ())), preferred_element_type=F32)

        def down(d, _):
            out = turned(acts[2, here, :], 2, d)
            grad = turned(acts[0, here, :], 0, d) + turned(acts[1, here, :], 1, d)
            for h in range(2):
                cols = slice(h * LANES, (h + 1) * LANES)
                wide[pl.ds(2 * d + h, group, stride=tall), :] = out[:, cols]
                wide[pl.ds(chunks + 2 * d + h, group, stride=tall), :] = grad[:, cols]
            return 0

        lax.fori_loop(0, chunks // 2, down, 0)
        rsend[pl.ds(dy * nz, nz)] = wide[...].astype(BF16).reshape(nz, CAP * tall, LANES)
        scatter(dy, rsend, rrecv, rs_sem, rr_sem, -1)
        return 0

    lax.fori_loop(0, ny, expert, 0)

    def partial(m, shard):
        return lax.dot_general(
            xo[m // 2, shard], acts[m], (((0,), (0,)), ((), ())), preferred_element_type=F32
        )

    def to_twin(i, _):
        dx, m = lax.rem(i // 3 + 1, nx), lax.rem(i, 3)
        csend[i] = partial(m, lax.rem(x + dx, nx) * 2 + 1 - core).astype(BF16)
        remote(csend.at[i], crecv.at[i], gcs_sem.at[i], gcr_sem.at[i], twin).start()
        return 0

    lax.fori_loop(0, 3 * nx, to_twin, 0)

    def along_x(i, _):
        dx, m = lax.rem(i // 3 + 1, nx), lax.rem(i, 3)
        total = partial(m, lax.rem(x + dx, nx) * 2 + core)
        remote(csend.at[i], crecv.at[i], gcs_sem.at[i], gcr_sem.at[i], twin).wait()
        total = total + crecv[i].astype(F32)

        @pl.when(dx > 0)
        def _():
            xsend[i] = total.astype(BF16)
            remote(xsend.at[i], xrecv.at[i], gxs_sem.at[i], gxr_sem.at[i], at_x(dx)).start()

        @pl.when(dx == 0)
        def _():
            acc[m] = total

        return 0

    lax.fori_loop(0, 3 * nx, along_x, 0)

    def returned(dy, _):
        remote(
            rrecv.at[pl.ds(dy * nz, nz)], rrecv.at[pl.ds(dy * nz, nz)], rs_sem, rr_sem.at[dy], twin
        ).wait_recv()
        unpack(rrecv, dy, back)
        return 0

    lax.fori_loop(0, ny - 1, returned, 0)

    def collect(i, _):
        remote(xsend.at[i], xrecv.at[i], gxs_sem.at[i], gxr_sem.at[i], at_x(lax.rem(i // 3 + 1, nx))).wait()
        m = lax.rem(i, 3)
        acc[m] = acc[m] + xrecv[i].astype(F32)
        return 0

    lax.fori_loop(0, 3 * (nx - 1), collect, 0)
    for m, out in enumerate((og, ou, od)):
        out[0] = acc[m]

    returned(jnp.int32(ny - 1), 0)

    total = ny * group
    lane = lax.broadcasted_iota(jnp.int32, (1, total), 1)
    lane_q = fifth(lane)
    wanted = slot_id(lane_q // nz, lane_q & (nz - 1), lane - CAP * lane_q)
    pick = [jnp.where(col_target[k] == wanted, 1.0, 0.0) for k in range(2)]
    both = (pick[0] + pick[1]).astype(BF16)
    pick = [p.astype(BF16) for p in pick]
    sums = [jnp.zeros((rows, 1), F32) for _ in range(2)]
    for c in range(chunks):
        cols = slice(c * LANES, (c + 1) * LANES)
        out = [jnp.dot(p, back[0, c], preferred_element_type=F32) for p in pick]
        mixed[:, cols] = (pr[0] * out[0] + pr[1] * out[1]).astype(BF16)
        gtok[:, cols] = jnp.dot(both, back[1, c], preferred_element_type=F32).astype(BF16)
        cot_c = cot[:, cols].astype(F32)
        sums = [s + jnp.sum(cot_c * o, axis=1, keepdims=True) for s, o in zip(sums, out)]
    for k in range(2):
        gprob[:, k:k + 1] = sums[k]

    count = ny * nz
    for buf, sem in ((send, fs_sem), (rsend, rs_sem)):
        rest = buf.at[pl.ds(1, count - 1)]
        remote(rest, rest, sem, fr_sem.at[0], twin).wait_send()
    for dx in range(nx):
        remote(mine, mine, wcs_sem.at[dx], wcr_sem.at[dx], twin).wait_send()
        if dx:
            remote(mine, mine, wxs_sem.at[dx], wxr_sem.at[dx], at_x(dx)).wait_send()


def per_device(nx, nz_lo, nz_hi, tokens, cotangent, gate_probs, expert_ids, gate_weight, up_weight, down_weight):
    rows, width = tokens.shape
    wide_n = gate_weight.shape[2]
    shard = gate_weight.shape[1]
    experts = nz_lo * nz_hi * NY
    chunks = width // LANES
    tall = 2 * chunks
    slots = experts * CAP
    message = (experts, CAP * tall, LANES)
    vmem = pl.BlockSpec(memory_space=pltpu.VMEM)
    anywhere = pl.BlockSpec(memory_space=pl.ANY)
    dma = pltpu.SemaphoreType.DMA
    grad = jax.ShapeDtypeStruct((1, shard, wide_n), F32)
    pieces = (3 * nx, shard, wide_n)
    return pl.pallas_call(
        functools.partial(kernel, nx, nz_lo, nz_hi, NY),
        out_shape=(
            jax.ShapeDtypeStruct((rows, width), BF16),
            jax.ShapeDtypeStruct((rows, width), BF16),
            jax.ShapeDtypeStruct((rows, 2), F32),
            grad, grad, grad,
        ),
        in_specs=[vmem] * 4 + [anywhere] * 3,
        out_specs=(vmem,) * 6,
        scratch_shapes=[
            pltpu.VMEM((3, 2 * nx, shard, wide_n), BF16),
            pltpu.VMEM(message, BF16),
            pltpu.VMEM(message, BF16),
            pltpu.VMEM(message, BF16),
            pltpu.VMEM(message, BF16),
            pltpu.VMEM((slots // NY * tall, LANES), F32),
            pltpu.VMEM((2, chunks, slots, LANES), BF16),
            pltpu.VMEM((3, slots, wide_n), BF16),
            pltpu.VMEM((2 * rows, width), BF16),
            pltpu.VMEM(pieces, BF16),
            pltpu.VMEM(pieces, BF16),
            pltpu.VMEM(pieces, BF16),
            pltpu.VMEM(pieces, BF16),
            pltpu.VMEM((3, shard, wide_n), F32),
            pltpu.VMEM((2, chunks, slots, LANES), BF16),
            dma((3,)), dma, dma((NY,)), dma, dma((NY,)),
            dma((nx,)), dma((nx,)), dma((nx,)), dma((nx,)),
            dma((3 * nx,)), dma((3 * nx,)), dma((3 * nx,)), dma((3 * nx,)),
        ],
        compiler_params=pltpu.CompilerParams(
            collective_id=0, has_side_effects=True, vmem_limit_bytes=56 * 2**20
        ),
    )(tokens, cotangent, gate_probs, expert_ids, gate_weight, up_weight, down_weight)


def solution(mesh):
    tokens = P(("dp", "expouter", "expinner"), None)
    weights = P(("expouter", "expinner"), "dp", None)
    nx = mesh.shape["dp"] // 2
    nz_lo = mesh.shape["expouter"]
    nz_hi = mesh.shape["expinner"] // NY
    return jax.shard_map(
        functools.partial(per_device, nx, nz_lo, nz_hi),
        mesh=mesh,
        in_specs=(tokens,) * 4 + (weights,) * 3,
        out_specs=(tokens,) * 3 + (weights,) * 3,
        check_vma=False,
    )
```

```python
import functools

import jax
import jax.numpy as jnp
from jax import lax
from jax.experimental import pallas as pl
from jax.experimental.pallas import tpu as pltpu
from jax.sharding import PartitionSpec as P

MESH = pl.DeviceIdType.MESH
F32 = jnp.float32
BF16 = jnp.bfloat16
LANES = 128
NY = 4
CAP = 5


def fifth(v):
    return (v * 52429) >> 18


def kernel(
    nx, nz_lo, nz_hi, ny,
    tok_in, cot_in, probs, ids, wg, wu, wd,
    mixed, gtok, gprob, og, ou, od,
    tok, cot, picked, weights, send, recv, rsend, rrecv, wide, xo, acts, scaled,
    csend, crecv, xsend, xrecv, acc, back,
    load_sem, store_sem, fs_sem, fr_sem, rs_sem, rr_sem,
    wxs_sem, wxr_sem, wcs_sem, wcr_sem,
    gcs_sem, gcr_sem, gxs_sem, gxr_sem,
):
    nz = nz_lo * nz_hi
    rows, width = tok.shape
    chunks = width // LANES
    tall = 2 * chunks
    group = nz * CAP
    hidden_n = wg.shape[2]
    me = lax.axis_index("dp")
    x, core = me // 2, me % 2
    inner = lax.axis_index("expinner")
    y = inner % ny
    z = (inner // ny) * nz_lo + lax.axis_index("expouter")

    def at_yz(dy, dz):
        tz = lax.rem(z + dz + nz, nz)
        ty = lax.rem(y + dy + ny, ny)
        return {"expouter": lax.rem(tz, nz_lo), "expinner": (tz // nz_lo) * ny + ty}

    def at_x(dx):
        return {"dp": lax.rem(x + dx, nx) * 2 + core}

    twin = {"dp": x * 2 + 1 - core}

    def remote(src, dst, ss, rs, device):
        return pltpu.make_async_remote_copy(
            src_ref=src, dst_ref=dst, send_sem=ss, recv_sem=rs,
            device_id=device, device_id_type=MESH,
        )

    loads = [
        pltpu.make_async_copy(a, b, load_sem.at[i])
        for i, (a, b) in enumerate(
            [(tok_in, tok), (cot_in, cot)]
            + [(w.at[0], weights.at[m, me]) for m, w in enumerate((wg, wu, wd))]
        )
    ]
    for copy in loads:
        copy.start()
    barrier = pltpu.get_barrier_semaphore()

    def greet(i, _):
        pl.semaphore_signal(barrier, inc=1, device_id=at_yz(i // nz, lax.rem(i, nz)), device_id_type=MESH)
        return 0

    lax.fori_loop(1, ny * nz, greet, 0)
    for dx in range(1, nx):
        pl.semaphore_signal(barrier, inc=1, device_id=at_x(dx), device_id_type=MESH)
    pl.semaphore_signal(barrier, inc=1, device_id=twin, device_id_type=MESH)

    idf = ids[...].astype(F32)
    over_id = [jnp.broadcast_to(idf[k:k + 1, :], (rows, rows)) for k in range(2)]
    down_id = [jnp.transpose(b) for b in over_id]
    first = lax.broadcasted_iota(jnp.int32, (rows, rows), 0)
    second = lax.broadcasted_iota(jnp.int32, (rows, rows), 1)
    col_target, row_target = [], []
    for k in range(2):
        hits = sum(jnp.where((down_id[k] == over_id[j]) & (second < first), 1.0, 0.0) for j in range(2))
        col_target.append(down_id[k][:, 0:1] * CAP + jnp.sum(hits, axis=1, keepdims=True))
        hits = sum(jnp.where((down_id[j] == over_id[k]) & (first < second), 1.0, 0.0) for j in range(2))
        row_target.append(idf[k:k + 1, :] * CAP + jnp.sum(hits, axis=0, keepdims=True))
    pr = [jnp.transpose(jnp.broadcast_to(probs[k:k + 1, :], (rows, rows)))[:, 0:1] for k in range(2)]
    for copy in loads[:2]:
        copy.wait()
    for k in range(2):
        scaled[k * rows:(k + 1) * rows, :] = (pr[k] * cot[...].astype(F32)).astype(BF16)

    def slot_id(dy, q, slot):
        tz = (z + q) & (nz - 1)
        ty = (y + dy) & (ny - 1)
        expert = (tz & (nz_lo - 1)) * (nz_hi * ny) + (tz // nz_lo) * ny + ty
        return (expert * CAP + slot).astype(F32)

    line = lax.broadcasted_iota(jnp.int32, (group, 1), 0)
    line_dz = fifth(line)
    line_slot = line - CAP * line_dz

    def pack(dy):
        wanted = slot_id(dy, line_dz, line_slot)
        sel = [jnp.where(wanted == row_target[k], 1.0, 0.0) for k in range(2)]
        both = (sel[0] + sel[1]).astype(BF16)
        each = jnp.concatenate(sel, axis=1).astype(BF16)
        rows_x = jnp.dot(both, tok[...], preferred_element_type=F32)
        rows_o = jnp.dot(each, scaled[...], preferred_element_type=F32)
        for c in range(chunks):
            cols = slice(c * LANES, (c + 1) * LANES)
            wide[pl.ds(c, group, stride=tall), :] = rows_x[:, cols]
            wide[pl.ds(chunks + c, group, stride=tall), :] = rows_o[:, cols]
        send[pl.ds(dy * nz, nz)] = wide[...].astype(BF16).reshape(nz, CAP * tall, LANES)

    def scatter(dy, src, dst, ss, rs, sign):
        def one(n, _):
            j = nz - 1 - n
            dz = jnp.where(lax.rem(j, 2) == 1, (j + 1) // 2, lax.rem(nz - j // 2, nz))
            i = dy * nz + dz

            @pl.when(i > 0)
            def _():
                remote(src.at[i], dst.at[i], ss, rs.at[dy], at_yz(sign * dy, sign * dz)).start()

            return 0

        lax.fori_loop(0, nz, one, 0)

        @pl.when(dy == 0)
        def _():
            pltpu.make_async_copy(src.at[0], dst.at[0], rs.at[0]).start()

    pack(jnp.int32(0))
    for copy in loads[2:]:
        copy.wait()
    pl.semaphore_wait(barrier, ny * nz - 1 + nx - 1 + 1)
    scatter(jnp.int32(0), send, recv, fs_sem, fr_sem, 1)

    mine = weights.at[:, me]
    remote(mine, mine, wcs_sem.at[0], wcr_sem.at[0], twin).start()
    for dx in range(1, nx):
        remote(mine, mine, wxs_sem.at[dx], wxr_sem.at[dx], at_x(dx)).start()

    def pack_and_send(dy, _):
        pack(dy)
        scatter(dy, send, recv, fs_sem, fr_sem, 1)
        return 0

    lax.fori_loop(1, ny, pack_and_send, 0)

    for dx in range(1, nx):
        theirs = weights.at[:, lax.rem(x - dx + nx, nx) * 2 + core]
        remote(theirs, theirs, wxs_sem.at[dx], wxr_sem.at[dx], at_x(dx)).wait_recv()
        remote(theirs, theirs, wcs_sem.at[dx], wcr_sem.at[dx], twin).start()
    for dx in range(nx):
        theirs = weights.at[:, lax.rem(x - dx + nx, nx) * 2 + 1 - core]
        remote(theirs, theirs, wcs_sem.at[dx], wcr_sem.at[dx], twin).wait_recv()

    def unpack(buf, dy, out):
        wide[...] = buf[pl.ds(dy * nz, nz)].reshape(nz * CAP * tall, LANES).astype(F32)
        here = pl.ds(pl.multiple_of(dy * group, 16), group)
        for part in range(2):
            for c in range(chunks):
                out[part, c, here, :] = wide[pl.ds(part * chunks + c, group, stride=tall), :].astype(BF16)

    step = 256

    def expert(dy, _):
        remote(
            recv.at[pl.ds(dy * nz, nz)], recv.at[pl.ds(dy * nz, nz)], fs_sem, fr_sem.at[dy], twin
        ).wait_recv()
        unpack(recv, dy, xo)
        here = pl.ds(pl.multiple_of(dy * group, 16), group)
        rows_x = jnp.concatenate([xo[0, c, here, :] for c in range(chunks)], axis=1)
        rows_o = jnp.concatenate([xo[1, c, here, :] for c in range(chunks)], axis=1)

        def up(n, _):
            cols = pl.ds(pl.multiple_of(n * step, step), step)
            gate = jnp.dot(rows_x, weights[0, :, :, cols].reshape(width, step), preferred_element_type=F32)
            lift = jnp.dot(rows_x, weights[1, :, :, cols].reshape(width, step), preferred_element_type=F32)
            grad = jnp.dot(rows_o, weights[2, :, :, cols].reshape(width, step), preferred_element_type=F32)
            sigma = jax.nn.sigmoid(gate)
            active = gate * sigma
            slope = sigma * (1.0 + gate * (1.0 - sigma))
            acts[0, here, cols] = (grad * lift * slope).astype(BF16)
            acts[1, here, cols] = (grad * active).astype(BF16)
            acts[2, here, cols] = (active * lift).astype(BF16)
            return 0

        lax.fori_loop(0, hidden_n // step, up, 0)

        def turned(a, m, d):
            w = weights[m, pl.ds(d * 2, 2)].reshape(2 * LANES, hidden_n)
            return lax.dot_general(a, w, (((1,), (1,)), ((), ())), preferred_element_type=F32)

        def down(d, _):
            out = turned(acts[2, here, :], 2, d)
            grad = turned(acts[0, here, :], 0, d) + turned(acts[1, here, :], 1, d)
            for h in range(2):
                cols = slice(h * LANES, (h + 1) * LANES)
                wide[pl.ds(2 * d + h, group, stride=tall), :] = out[:, cols]
                wide[pl.ds(chunks + 2 * d + h, group, stride=tall), :] = grad[:, cols]
            return 0

        lax.fori_loop(0, chunks // 2, down, 0)
        rsend[pl.ds(dy * nz, nz)] = wide[...].astype(BF16).reshape(nz, CAP * tall, LANES)
        scatter(dy, rsend, rrecv, rs_sem, rr_sem, -1)
        return 0

    lax.fori_loop(0, ny, expert, 0)

    def partial(m, shard):
        return lax.dot_general(
            xo[m // 2, shard], acts[m], (((0,), (0,)), ((), ())), preferred_element_type=F32
        )

    def to_twin(i, _):
        dx, m = lax.rem(i // 3 + 1, nx), lax.rem(i, 3)
        csend[i] = partial(m, lax.rem(x + dx, nx) * 2 + 1 - core).astype(BF16)
        remote(csend.at[i], crecv.at[i], gcs_sem.at[i], gcr_sem.at[i], twin).start()
        return 0

    lax.fori_loop(0, 3 * nx, to_twin, 0)

    def along_x(i, _):
        dx, m = lax.rem(i // 3 + 1, nx), lax.rem(i, 3)
        total = partial(m, lax.rem(x + dx, nx) * 2 + core)
        remote(csend.at[i], crecv.at[i], gcs_sem.at[i], gcr_sem.at[i], twin).wait()
        total = total + crecv[i].astype(F32)

        @pl.when(dx > 0)
        def _():
            xsend[i] = total.astype(BF16)
            remote(xsend.at[i], xrecv.at[i], gxs_sem.at[i], gxr_sem.at[i], at_x(dx)).start()

        @pl.when(dx == 0)
        def _():
            acc[m] = total

        return 0

    lax.fori_loop(0, 3 * nx, along_x, 0)

    def returned(dy, _):
        remote(
            rrecv.at[pl.ds(dy * nz, nz)], rrecv.at[pl.ds(dy * nz, nz)], rs_sem, rr_sem.at[dy], twin
        ).wait_recv()
        unpack(rrecv, dy, back)
        return 0

    lax.fori_loop(0, ny - 1, returned, 0)

    early = (ny - 1) * group

    def chosen(start, count):
        lane = lax.broadcasted_iota(jnp.int32, (1, count), 1) + start
        lane_q = fifth(lane)
        wanted = slot_id(lane_q // nz, lane_q & (nz - 1), lane - CAP * lane_q)
        pick = [jnp.where(col_target[k] == wanted, 1.0, 0.0) for k in range(2)]
        return [p.astype(BF16) for p in (pick[0], pick[1], pick[0] + pick[1])]

    def gather(pick, here, c):
        return [jnp.dot(p, back[part, c, here, :], preferred_element_type=F32) for p, part in zip(pick, (0, 0, 1))]

    pick = chosen(0, early)
    for c in range(chunks):
        for k, value in enumerate(gather(pick, slice(0, early), c)):
            picked[k, :, c * LANES:(c + 1) * LANES] = value

    def collect(i, _):
        remote(xsend.at[i], xrecv.at[i], gxs_sem.at[i], gxr_sem.at[i], at_x(lax.rem(i // 3 + 1, nx))).wait()
        m = lax.rem(i, 3)
        acc[m] = acc[m] + xrecv[i].astype(F32)
        return 0

    lax.fori_loop(0, 3 * (nx - 1), collect, 0)
    stores = [pltpu.make_async_copy(acc.at[m], out.at[0], store_sem.at[m]) for m, out in enumerate((og, ou, od))]
    for copy in stores:
        copy.start()

    returned(jnp.int32(ny - 1), 0)
    pick = chosen(early, group)
    sums = [jnp.zeros((rows, 1), F32) for _ in range(2)]
    for c in range(chunks):
        cols = slice(c * LANES, (c + 1) * LANES)
        out = [picked[k, :, cols] + value for k, value in enumerate(gather(pick, slice(early, early + group), c))]
        mixed[:, cols] = (pr[0] * out[0] + pr[1] * out[1]).astype(BF16)
        gtok[:, cols] = out[2].astype(BF16)
        cot_c = cot[:, cols].astype(F32)
        sums = [s + jnp.sum(cot_c * o, axis=1, keepdims=True) for s, o in zip(sums, out)]
    for k in range(2):
        gprob[k:k + 1, :] = jnp.transpose(jnp.broadcast_to(sums[k], (rows, rows)))[0:1, :]

    for copy in stores:
        copy.wait()

    count = ny * nz
    for buf, sem in ((send, fs_sem), (rsend, rs_sem)):
        rest = buf.at[pl.ds(1, count - 1)]
        remote(rest, rest, sem, fr_sem.at[0], twin).wait_send()
    for dx in range(nx):
        remote(mine, mine, wcs_sem.at[dx], wcr_sem.at[dx], twin).wait_send()
        if dx:
            remote(mine, mine, wxs_sem.at[dx], wxr_sem.at[dx], at_x(dx)).wait_send()


def hand_over(*refs):
    count = len(refs) // 3
    sems = refs[-1]
    into = [pltpu.make_async_copy(refs[i], refs[2 * count + i], sems.at[0, i]) for i in range(count)]
    out = [pltpu.make_async_copy(refs[2 * count + i], refs[count + i], sems.at[1, i]) for i in range(count)]
    for copy in into:
        copy.start()
    for first, second in zip(into, out):
        first.wait()
        second.start()
    for copy in out:
        copy.wait()


def per_device(nx, nz_lo, nz_hi, tokens, cotangent, gate_probs, expert_ids, gate_weight, up_weight, down_weight):
    rows, width = tokens.shape
    wide_n = gate_weight.shape[2]
    shard = gate_weight.shape[1]
    experts = nz_lo * nz_hi * NY
    chunks = width // LANES
    tall = 2 * chunks
    slots = experts * CAP
    message = (experts, CAP * tall, LANES)
    vmem = pl.BlockSpec(memory_space=pltpu.VMEM)
    anywhere = pl.BlockSpec(memory_space=pl.ANY)
    dma = pltpu.SemaphoreType.DMA
    grad = jax.ShapeDtypeStruct((1, shard, wide_n), F32)
    pieces = (3 * nx, shard, wide_n)
    shapes = (
        jax.ShapeDtypeStruct((rows, width), BF16),
        jax.ShapeDtypeStruct((rows, width), BF16),
        jax.ShapeDtypeStruct((2, rows), F32),
        grad, grad, grad,
    )
    results = pl.pallas_call(
        functools.partial(kernel, nx, nz_lo, nz_hi, NY),
        out_shape=shapes,
        in_specs=[anywhere] * 2 + [vmem] * 2 + [anywhere] * 3,
        out_specs=(vmem,) * 3 + (anywhere,) * 3,
        scratch_shapes=[
            pltpu.VMEM((rows, width), BF16),
            pltpu.VMEM((rows, width), BF16),
            pltpu.VMEM((3, rows, width), F32),
            pltpu.VMEM((3, 2 * nx, shard, wide_n), BF16),
            pltpu.VMEM(message, BF16),
            pltpu.VMEM(message, BF16),
            pltpu.VMEM(message, BF16),
            pltpu.VMEM(message, BF16),
            pltpu.VMEM((slots // NY * tall, LANES), F32),
            pltpu.VMEM((2, chunks, slots, LANES), BF16),
            pltpu.VMEM((3, slots, wide_n), BF16),
            pltpu.VMEM((2 * rows, width), BF16),
            pltpu.VMEM(pieces, BF16),
            pltpu.VMEM(pieces, BF16),
            pltpu.VMEM(pieces, BF16),
            pltpu.VMEM(pieces, BF16),
            pltpu.VMEM((3, shard, wide_n), F32),
            pltpu.VMEM((2, chunks, slots, LANES), BF16),
            dma((5,)), dma((3,)), dma, dma((NY,)), dma, dma((NY,)),
            dma((nx,)), dma((nx,)), dma((nx,)), dma((nx,)),
            dma((3 * nx,)), dma((3 * nx,)), dma((3 * nx,)), dma((3 * nx,)),
        ],
        compiler_params=pltpu.CompilerParams(
            collective_id=0, has_side_effects=True, vmem_limit_bytes=56 * 2**20
        ),
    )(tokens, cotangent, gate_probs.T, expert_ids.T, gate_weight, up_weight, down_weight)
    mixed, gtok, gprob, *grads = pl.pallas_call(
        hand_over,
        out_shape=shapes,
        in_specs=[anywhere] * 6,
        out_specs=(anywhere,) * 6,
        scratch_shapes=[pltpu.VMEM(a.shape, a.dtype) for a in shapes] + [dma((2, 6))],
    )(*results)
    return (mixed, gtok, gprob.T, *grads)


def solution(mesh):
    tokens = P(("dp", "expouter", "expinner"), None)
    weights = P(("expouter", "expinner"), "dp", None)
    nx = mesh.shape["dp"] // 2
    nz_lo = mesh.shape["expouter"]
    nz_hi = mesh.shape["expinner"] // NY
    return jax.shard_map(
        functools.partial(per_device, nx, nz_lo, nz_hi),
        mesh=mesh,
        in_specs=(tokens,) * 4 + (weights,) * 3,
        out_specs=(tokens,) * 3 + (weights,) * 3,
        check_vma=False,
    )
```

```python
import functools

import jax
import jax.numpy as jnp
from jax import lax
from jax.experimental import pallas as pl
from jax.experimental.pallas import tpu as pltpu
from jax.sharding import PartitionSpec as P

MESH = pl.DeviceIdType.MESH
F32 = jnp.float32
BF16 = jnp.bfloat16
LANES = 128
NY = 4
CAP = 5


def fifth(v):
    return (v * 52429) >> 18


def kernel(
    nx, nz_lo, nz_hi, ny,
    tok_in, cot_in, probs, ids, wg, wu, wd,
    mixed, gtok, gprob, og, ou, od,
    tok, cot, picked, weights, send, recv, rsend, rrecv, wide, xo, acts, scaled,
    csend, crecv, xsend, xrecv, acc, back,
    load_sem, store_sem, fs_sem, fr_sem, rs_sem, rr_sem,
    wxs_sem, wxr_sem, wcs_sem, wcr_sem,
    gcs_sem, gcr_sem, gxs_sem, gxr_sem,
):
    nz = nz_lo * nz_hi
    rows, width = tok.shape
    chunks = width // LANES
    tall = 2 * chunks
    group = nz * CAP
    hidden_n = wg.shape[2]
    me = lax.axis_index("dp")
    x, core = me // 2, me % 2
    inner = lax.axis_index("expinner")
    y = inner % ny
    z = (inner // ny) * nz_lo + lax.axis_index("expouter")

    def at_yz(dy, dz):
        tz = lax.rem(z + dz + nz, nz)
        ty = lax.rem(y + dy + ny, ny)
        return {"expouter": lax.rem(tz, nz_lo), "expinner": (tz // nz_lo) * ny + ty}

    def at_x(dx):
        return {"dp": lax.rem(x + dx, nx) * 2 + core}

    twin = {"dp": x * 2 + 1 - core}

    def remote(src, dst, ss, rs, device):
        return pltpu.make_async_remote_copy(
            src_ref=src, dst_ref=dst, send_sem=ss, recv_sem=rs,
            device_id=device, device_id_type=MESH,
        )

    loads = [
        pltpu.make_async_copy(a, b, load_sem.at[i])
        for i, (a, b) in enumerate(
            [(tok_in, tok), (cot_in, cot)]
            + [(w.at[0], weights.at[m, me]) for m, w in enumerate((wg, wu, wd))]
        )
    ]
    for copy in loads:
        copy.start()
    barrier = pltpu.get_barrier_semaphore()

    def greet(i, _):
        pl.semaphore_signal(barrier, inc=1, device_id=at_yz(i // nz, lax.rem(i, nz)), device_id_type=MESH)
        return 0

    lax.fori_loop(1, ny * nz, greet, 0)
    for dx in range(1, nx):
        pl.semaphore_signal(barrier, inc=1, device_id=at_x(dx), device_id_type=MESH)
    pl.semaphore_signal(barrier, inc=1, device_id=twin, device_id_type=MESH)

    idf = ids[...].astype(F32)
    over_id = [jnp.broadcast_to(idf[k:k + 1, :], (rows, rows)) for k in range(2)]
    down_id = [jnp.transpose(b) for b in over_id]
    first = lax.broadcasted_iota(jnp.int32, (rows, rows), 0)
    second = lax.broadcasted_iota(jnp.int32, (rows, rows), 1)
    col_target, row_target = [], []
    for k in range(2):
        hits = sum(jnp.where((down_id[k] == over_id[j]) & (second < first), 1.0, 0.0) for j in range(2))
        col_target.append(down_id[k][:, 0:1] * CAP + jnp.sum(hits, axis=1, keepdims=True))
        hits = sum(jnp.where((down_id[j] == over_id[k]) & (first < second), 1.0, 0.0) for j in range(2))
        row_target.append(idf[k:k + 1, :] * CAP + jnp.sum(hits, axis=0, keepdims=True))
    pr = [jnp.transpose(jnp.broadcast_to(probs[k:k + 1, :], (rows, rows)))[:, 0:1] for k in range(2)]
    for copy in loads[:2]:
        copy.wait()
    for k in range(2):
        scaled[k * rows:(k + 1) * rows, :] = (pr[k] * cot[...].astype(F32)).astype(BF16)

    def slot_id(dy, q, slot):
        tz = (z + q) & (nz - 1)
        ty = (y + dy) & (ny - 1)
        expert = (tz & (nz_lo - 1)) * (nz_hi * ny) + (tz // nz_lo) * ny + ty
        return (expert * CAP + slot).astype(F32)

    line = lax.broadcasted_iota(jnp.int32, (group, 1), 0)
    line_dz = fifth(line)
    line_slot = line - CAP * line_dz

    def pack(dy):
        wanted = slot_id(dy, line_dz, line_slot)
        sel = [jnp.where(wanted == row_target[k], 1.0, 0.0) for k in range(2)]
        both = (sel[0] + sel[1]).astype(BF16)
        each = jnp.concatenate(sel, axis=1).astype(BF16)
        rows_x = jnp.dot(both, tok[...], preferred_element_type=F32)
        rows_o = jnp.dot(each, scaled[...], preferred_element_type=F32)
        for c in range(chunks):
            cols = slice(c * LANES, (c + 1) * LANES)
            wide[pl.ds(c, group, stride=tall), :] = rows_x[:, cols]
            wide[pl.ds(chunks + c, group, stride=tall), :] = rows_o[:, cols]
        send[pl.ds(dy * nz, nz)] = wide[...].astype(BF16).reshape(nz, CAP * tall, LANES)

    def scatter(dy, src, dst, ss, rs, sign):
        def one(n, _):
            j = nz - 1 - n
            dz = jnp.where(lax.rem(j, 2) == 1, (j + 1) // 2, lax.rem(nz - j // 2, nz))
            if sign < 0:
                dz = lax.rem(z - n + nz, nz)
            i = dy * nz + dz

            @pl.when(i > 0)
            def _():
                remote(src.at[i], dst.at[i], ss, rs.at[dy], at_yz(sign * dy, sign * dz)).start()

            return 0

        lax.fori_loop(0, nz, one, 0)

        @pl.when(dy == 0)
        def _():
            pltpu.make_async_copy(src.at[0], dst.at[0], rs.at[0]).start()

    pack(jnp.int32(0))
    for copy in loads[2:]:
        copy.wait()
    pl.semaphore_wait(barrier, ny * nz - 1 + nx - 1 + 1)
    scatter(jnp.int32(0), send, recv, fs_sem, fr_sem, 1)

    mine = weights.at[:, me]
    remote(mine, mine, wcs_sem.at[0], wcr_sem.at[0], twin).start()
    for dx in range(1, nx):
        remote(mine, mine, wxs_sem.at[dx], wxr_sem.at[dx], at_x(dx)).start()

    def pack_and_send(dy, _):
        pack(dy)
        scatter(dy, send, recv, fs_sem, fr_sem, 1)
        return 0

    lax.fori_loop(1, ny, pack_and_send, 0)

    for dx in range(1, nx):
        theirs = weights.at[:, lax.rem(x - dx + nx, nx) * 2 + core]
        remote(theirs, theirs, wxs_sem.at[dx], wxr_sem.at[dx], at_x(dx)).wait_recv()
        remote(theirs, theirs, wcs_sem.at[dx], wcr_sem.at[dx], twin).start()
    for dx in range(nx):
        theirs = weights.at[:, lax.rem(x - dx + nx, nx) * 2 + 1 - core]
        remote(theirs, theirs, wcs_sem.at[dx], wcr_sem.at[dx], twin).wait_recv()

    def unpack(buf, dy, out):
        wide[...] = buf[pl.ds(dy * nz, nz)].reshape(nz * CAP * tall, LANES).astype(F32)
        here = pl.ds(pl.multiple_of(dy * group, 16), group)
        for part in range(2):
            for c in range(chunks):
                out[part, c, here, :] = wide[pl.ds(part * chunks + c, group, stride=tall), :].astype(BF16)

    step = 256

    def expert(dy, _):
        remote(
            recv.at[pl.ds(dy * nz, nz)], recv.at[pl.ds(dy * nz, nz)], fs_sem, fr_sem.at[dy], twin
        ).wait_recv()
        unpack(recv, dy, xo)
        here = pl.ds(pl.multiple_of(dy * group, 16), group)
        rows_x = jnp.concatenate([xo[0, c, here, :] for c in range(chunks)], axis=1)
        rows_o = jnp.concatenate([xo[1, c, here, :] for c in range(chunks)], axis=1)

        def up(n, _):
            cols = pl.ds(pl.multiple_of(n * step, step), step)
            gate = jnp.dot(rows_x, weights[0, :, :, cols].reshape(width, step), preferred_element_type=F32)
            lift = jnp.dot(rows_x, weights[1, :, :, cols].reshape(width, step), preferred_element_type=F32)
            grad = jnp.dot(rows_o, weights[2, :, :, cols].reshape(width, step), preferred_element_type=F32)
            sigma = jax.nn.sigmoid(gate)
            active = gate * sigma
            slope = sigma * (1.0 + gate * (1.0 - sigma))
            acts[0, here, cols] = (grad * lift * slope).astype(BF16)
            acts[1, here, cols] = (grad * active).astype(BF16)
            acts[2, here, cols] = (active * lift).astype(BF16)
            return 0

        lax.fori_loop(0, hidden_n // step, up, 0)

        def turned(a, m, d):
            w = weights[m, pl.ds(d * 2, 2)].reshape(2 * LANES, hidden_n)
            return lax.dot_general(a, w, (((1,), (1,)), ((), ())), preferred_element_type=F32)

        def down(d, _):
            out = turned(acts[2, here, :], 2, d)
            grad = turned(acts[0, here, :], 0, d) + turned(acts[1, here, :], 1, d)
            for h in range(2):
                cols = slice(h * LANES, (h + 1) * LANES)
                wide[pl.ds(2 * d + h, group, stride=tall), :] = out[:, cols]
                wide[pl.ds(chunks + 2 * d + h, group, stride=tall), :] = grad[:, cols]
            return 0

        lax.fori_loop(0, chunks // 2, down, 0)
        rsend[pl.ds(dy * nz, nz)] = wide[...].astype(BF16).reshape(nz, CAP * tall, LANES)
        scatter(dy, rsend, rrecv, rs_sem, rr_sem, -1)
        return 0

    lax.fori_loop(0, ny, expert, 0)

    def partial(m, shard):
        return lax.dot_general(
            xo[m // 2, shard], acts[m], (((0,), (0,)), ((), ())), preferred_element_type=F32
        )

    def to_twin(i, _):
        dx, m = lax.rem(i // 3 + 1, nx), lax.rem(i, 3)
        csend[i] = partial(m, lax.rem(x + dx, nx) * 2 + 1 - core).astype(BF16)
        remote(csend.at[i], crecv.at[i], gcs_sem.at[i], gcr_sem.at[i], twin).start()
        return 0

    lax.fori_loop(0, 3 * nx, to_twin, 0)

    def along_x(i, _):
        dx, m = lax.rem(i // 3 + 1, nx), lax.rem(i, 3)
        total = partial(m, lax.rem(x + dx, nx) * 2 + core)
        remote(csend.at[i], crecv.at[i], gcs_sem.at[i], gcr_sem.at[i], twin).wait()
        total = total + crecv[i].astype(F32)

        @pl.when(dx > 0)
        def _():
            xsend[i] = total.astype(BF16)
            remote(xsend.at[i], xrecv.at[i], gxs_sem.at[i], gxr_sem.at[i], at_x(dx)).start()

        @pl.when(dx == 0)
        def _():
            acc[m] = total

        return 0

    lax.fori_loop(0, 3 * nx, along_x, 0)

    def returned(dy, _):
        remote(
            rrecv.at[pl.ds(dy * nz, nz)], rrecv.at[pl.ds(dy * nz, nz)], rs_sem, rr_sem.at[dy], twin
        ).wait_recv()
        unpack(rrecv, dy, back)
        return 0

    lax.fori_loop(0, ny - 1, returned, 0)

    early = (ny - 1) * group

    def chosen(start, count):
        lane = lax.broadcasted_iota(jnp.int32, (1, count), 1) + start
        lane_q = fifth(lane)
        wanted = slot_id(lane_q // nz, lane_q & (nz - 1), lane - CAP * lane_q)
        pick = [jnp.where(col_target[k] == wanted, 1.0, 0.0) for k in range(2)]
        return [p.astype(BF16) for p in (pick[0], pick[1], pick[0] + pick[1])]

    def gather(pick, here, c):
        return [jnp.dot(p, back[part, c, here, :], preferred_element_type=F32) for p, part in zip(pick, (0, 0, 1))]

    pick = chosen(0, early)
    for c in range(chunks):
        for k, value in enumerate(gather(pick, slice(0, early), c)):
            picked[k, :, c * LANES:(c + 1) * LANES] = value

    def collect(i, _):
        remote(xsend.at[i], xrecv.at[i], gxs_sem.at[i], gxr_sem.at[i], at_x(lax.rem(i // 3 + 1, nx))).wait()
        m = lax.rem(i, 3)
        acc[m] = acc[m] + xrecv[i].astype(F32)
        return 0

    lax.fori_loop(0, 3 * (nx - 1), collect, 0)
    stores = [pltpu.make_async_copy(acc.at[m], out.at[0], store_sem.at[m]) for m, out in enumerate((og, ou, od))]
    for copy in stores:
        copy.start()

    returned(jnp.int32(ny - 1), 0)
    pick = chosen(early, group)
    sums = [jnp.zeros((rows, 1), F32) for _ in range(2)]
    for c in range(chunks):
        cols = slice(c * LANES, (c + 1) * LANES)
        out = [picked[k, :, cols] + value for k, value in enumerate(gather(pick, slice(early, early + group), c))]
        mixed[:, cols] = (pr[0] * out[0] + pr[1] * out[1]).astype(BF16)
        gtok[:, cols] = out[2].astype(BF16)
        cot_c = cot[:, cols].astype(F32)
        sums = [s + jnp.sum(cot_c * o, axis=1, keepdims=True) for s, o in zip(sums, out)]
    for k in range(2):
        gprob[k:k + 1, :] = jnp.transpose(jnp.broadcast_to(sums[k], (rows, rows)))[0:1, :]

    for copy in stores:
        copy.wait()

    count = ny * nz
    for buf, sem in ((send, fs_sem), (rsend, rs_sem)):
        rest = buf.at[pl.ds(1, count - 1)]
        remote(rest, rest, sem, fr_sem.at[0], twin).wait_send()
    for dx in range(nx):
        remote(mine, mine, wcs_sem.at[dx], wcr_sem.at[dx], twin).wait_send()
        if dx:
            remote(mine, mine, wxs_sem.at[dx], wxr_sem.at[dx], at_x(dx)).wait_send()


def hand_over(*refs):
    count = len(refs) // 3
    sems = refs[-1]
    into = [pltpu.make_async_copy(refs[i], refs[2 * count + i], sems.at[0, i]) for i in range(count)]
    out = [pltpu.make_async_copy(refs[2 * count + i], refs[count + i], sems.at[1, i]) for i in range(count)]
    for copy in into:
        copy.start()
    for first, second in zip(into, out):
        first.wait()
        second.start()
    for copy in out:
        copy.wait()


def per_device(nx, nz_lo, nz_hi, tokens, cotangent, gate_probs, expert_ids, gate_weight, up_weight, down_weight):
    rows, width = tokens.shape
    wide_n = gate_weight.shape[2]
    shard = gate_weight.shape[1]
    experts = nz_lo * nz_hi * NY
    chunks = width // LANES
    tall = 2 * chunks
    slots = experts * CAP
    message = (experts, CAP * tall, LANES)
    vmem = pl.BlockSpec(memory_space=pltpu.VMEM)
    anywhere = pl.BlockSpec(memory_space=pl.ANY)
    dma = pltpu.SemaphoreType.DMA
    grad = jax.ShapeDtypeStruct((1, shard, wide_n), F32)
    pieces = (3 * nx, shard, wide_n)
    shapes = (
        jax.ShapeDtypeStruct((rows, width), BF16),
        jax.ShapeDtypeStruct((rows, width), BF16),
        jax.ShapeDtypeStruct((2, rows), F32),
        grad, grad, grad,
    )
    results = pl.pallas_call(
        functools.partial(kernel, nx, nz_lo, nz_hi, NY),
        out_shape=shapes,
        in_specs=[anywhere] * 2 + [vmem] * 2 + [anywhere] * 3,
        out_specs=(vmem,) * 3 + (anywhere,) * 3,
        scratch_shapes=[
            pltpu.VMEM((rows, width), BF16),
            pltpu.VMEM((rows, width), BF16),
            pltpu.VMEM((3, rows, width), F32),
            pltpu.VMEM((3, 2 * nx, shard, wide_n), BF16),
            pltpu.VMEM(message, BF16),
            pltpu.VMEM(message, BF16),
            pltpu.VMEM(message, BF16),
            pltpu.VMEM(message, BF16),
            pltpu.VMEM((slots // NY * tall, LANES), F32),
            pltpu.VMEM((2, chunks, slots, LANES), BF16),
            pltpu.VMEM((3, slots, wide_n), BF16),
            pltpu.VMEM((2 * rows, width), BF16),
            pltpu.VMEM(pieces, BF16),
            pltpu.VMEM(pieces, BF16),
            pltpu.VMEM(pieces, BF16),
            pltpu.VMEM(pieces, BF16),
            pltpu.VMEM((3, shard, wide_n), F32),
            pltpu.VMEM((2, chunks, slots, LANES), BF16),
            dma((5,)), dma((3,)), dma, dma((NY,)), dma, dma((NY,)),
            dma((nx,)), dma((nx,)), dma((nx,)), dma((nx,)),
            dma((3 * nx,)), dma((3 * nx,)), dma((3 * nx,)), dma((3 * nx,)),
        ],
        compiler_params=pltpu.CompilerParams(
            collective_id=0, has_side_effects=True, vmem_limit_bytes=56 * 2**20
        ),
    )(tokens, cotangent, gate_probs.T, expert_ids.T, gate_weight, up_weight, down_weight)
    mixed, gtok, gprob, *grads = pl.pallas_call(
        hand_over,
        out_shape=shapes,
        in_specs=[anywhere] * 6,
        out_specs=(anywhere,) * 6,
        scratch_shapes=[pltpu.VMEM(a.shape, a.dtype) for a in shapes] + [dma((2, 6))],
    )(*results)
    return (mixed, gtok, gprob.T, *grads)


def solution(mesh):
    tokens = P(("dp", "expouter", "expinner"), None)
    weights = P(("expouter", "expinner"), "dp", None)
    nx = mesh.shape["dp"] // 2
    nz_lo = mesh.shape["expouter"]
    nz_hi = mesh.shape["expinner"] // NY
    return jax.shard_map(
        functools.partial(per_device, nx, nz_lo, nz_hi),
        mesh=mesh,
        in_specs=(tokens,) * 4 + (weights,) * 3,
        out_specs=(tokens,) * 3 + (weights,) * 3,
        check_vma=False,
    )
```

```python
import functools

import jax
import jax.numpy as jnp
from jax import lax
from jax.experimental import pallas as pl
from jax.experimental.pallas import tpu as pltpu
from jax.sharding import PartitionSpec as P

MESH = pl.DeviceIdType.MESH
F32 = jnp.float32
BF16 = jnp.bfloat16
LANES = 128
NY = 4
CAP = 5


def fifth(v):
    return (v * 52429) >> 18


def kernel(
    nx, nz_lo, nz_hi, ny,
    tok_in, cot_in, probs, ids, wg, wu, wd,
    mixed, gtok, gprob, og, ou, od,
    tok, cot, picked, weights, send, recv, rsend, rrecv, wide, xo, acts, scaled,
    csend, crecv, xsend, xrecv, acc, back,
    load_sem, store_sem, fs_sem, fr_sem, rs_sem, rr_sem,
    wxs_sem, wxr_sem, wcs_sem, wcr_sem,
    gcs_sem, gcr_sem, gxs_sem, gxr_sem,
):
    nz = nz_lo * nz_hi
    rows, width = tok.shape
    chunks = width // LANES
    tall = 2 * chunks
    group = nz * CAP
    hidden_n = wg.shape[2]
    me = lax.axis_index("dp")
    x, core = me // 2, me % 2
    inner = lax.axis_index("expinner")
    y = inner % ny
    z = (inner // ny) * nz_lo + lax.axis_index("expouter")

    def at_yz(dy, dz):
        tz = lax.rem(z + dz + nz, nz)
        ty = lax.rem(y + dy + ny, ny)
        return {"expouter": lax.rem(tz, nz_lo), "expinner": (tz // nz_lo) * ny + ty}

    def at_x(dx):
        return {"dp": lax.rem(x + dx, nx) * 2 + core}

    twin = {"dp": x * 2 + 1 - core}

    def remote(src, dst, ss, rs, device):
        return pltpu.make_async_remote_copy(
            src_ref=src, dst_ref=dst, send_sem=ss, recv_sem=rs,
            device_id=device, device_id_type=MESH,
        )

    loads = [
        pltpu.make_async_copy(a, b, load_sem.at[i])
        for i, (a, b) in enumerate(
            [(tok_in, tok), (cot_in, cot)]
            + [(w.at[0], weights.at[m, me]) for m, w in enumerate((wg, wu, wd))]
        )
    ]
    for copy in loads:
        copy.start()
    barrier = pltpu.get_barrier_semaphore()

    for dz in sorted(range(nz), key=lambda d: -min(d, nz - d)):
        for dy in range(ny):
            if dy or dz:
                tz = (z + dz) & (nz - 1)
                ty = (y + dy) & (ny - 1)
                there = {"expouter": tz & (nz_lo - 1), "expinner": (tz // nz_lo) * ny + ty}
                pl.semaphore_signal(barrier, inc=1, device_id=there, device_id_type=MESH)
    for dx in range(1, nx):
        pl.semaphore_signal(barrier, inc=1, device_id=at_x(dx), device_id_type=MESH)
    pl.semaphore_signal(barrier, inc=1, device_id=twin, device_id_type=MESH)

    idf = ids[...].astype(F32)
    over_id = [jnp.broadcast_to(idf[k:k + 1, :], (rows, rows)) for k in range(2)]
    down_id = [jnp.transpose(b) for b in over_id]
    first = lax.broadcasted_iota(jnp.int32, (rows, rows), 0)
    second = lax.broadcasted_iota(jnp.int32, (rows, rows), 1)
    col_target, row_target = [], []
    for k in range(2):
        hits = sum(jnp.where((down_id[k] == over_id[j]) & (second < first), 1.0, 0.0) for j in range(2))
        col_target.append(down_id[k][:, 0:1] * CAP + jnp.sum(hits, axis=1, keepdims=True))
        hits = sum(jnp.where((down_id[j] == over_id[k]) & (first < second), 1.0, 0.0) for j in range(2))
        row_target.append(idf[k:k + 1, :] * CAP + jnp.sum(hits, axis=0, keepdims=True))
    pr = [jnp.transpose(jnp.broadcast_to(probs[k:k + 1, :], (rows, rows)))[:, 0:1] for k in range(2)]
    for copy in loads[:2]:
        copy.wait()
    for k in range(2):
        scaled[k * rows:(k + 1) * rows, :] = (pr[k] * cot[...].astype(F32)).astype(BF16)

    def slot_id(dy, q, slot):
        tz = (z + q) & (nz - 1)
        ty = (y + dy) & (ny - 1)
        expert = (tz & (nz_lo - 1)) * (nz_hi * ny) + (tz // nz_lo) * ny + ty
        return (expert * CAP + slot).astype(F32)

    line = lax.broadcasted_iota(jnp.int32, (group, 1), 0)
    line_dz = fifth(line)
    line_slot = line - CAP * line_dz

    def pack(dy):
        wanted = slot_id(dy, line_dz, line_slot)
        sel = [jnp.where(wanted == row_target[k], 1.0, 0.0) for k in range(2)]
        both = (sel[0] + sel[1]).astype(BF16)
        each = jnp.concatenate(sel, axis=1).astype(BF16)
        rows_x = jnp.dot(both, tok[...], preferred_element_type=F32)
        rows_o = jnp.dot(each, scaled[...], preferred_element_type=F32)
        for c in range(chunks):
            cols = slice(c * LANES, (c + 1) * LANES)
            wide[pl.ds(c, group, stride=tall), :] = rows_x[:, cols]
            wide[pl.ds(chunks + c, group, stride=tall), :] = rows_o[:, cols]
        send[pl.ds(dy * nz, nz)] = wide[...].astype(BF16).reshape(nz, CAP * tall, LANES)

    def scatter(dy, src, dst, ss, rs, sign):
        def one(n, _):
            j = nz - 1 - n
            dz = jnp.where(lax.rem(j, 2) == 1, (j + 1) // 2, lax.rem(nz - j // 2, nz))
            if sign < 0:
                dz = lax.rem(z - n + nz, nz)
            i = dy * nz + dz

            @pl.when(i > 0)
            def _():
                remote(src.at[i], dst.at[i], ss, rs.at[dy], at_yz(sign * dy, sign * dz)).start()

            return 0

        lax.fori_loop(0, nz, one, 0)

        @pl.when(dy == 0)
        def _():
            pltpu.make_async_copy(src.at[0], dst.at[0], rs.at[0]).start()

    pack(jnp.int32(0))
    for copy in loads[2:]:
        copy.wait()
    pl.semaphore_wait(barrier, ny * nz - 1 + nx - 1 + 1)
    scatter(jnp.int32(0), send, recv, fs_sem, fr_sem, 1)

    mine = weights.at[:, me]
    remote(mine, mine, wcs_sem.at[0], wcr_sem.at[0], twin).start()
    for dx in range(1, nx):
        remote(mine, mine, wxs_sem.at[dx], wxr_sem.at[dx], at_x(dx)).start()

    def pack_and_send(dy, _):
        pack(dy)
        scatter(dy, send, recv, fs_sem, fr_sem, 1)
        return 0

    lax.fori_loop(1, ny, pack_and_send, 0)

    for dx in range(1, nx):
        theirs = weights.at[:, lax.rem(x - dx + nx, nx) * 2 + core]
        remote(theirs, theirs, wxs_sem.at[dx], wxr_sem.at[dx], at_x(dx)).wait_recv()
        remote(theirs, theirs, wcs_sem.at[dx], wcr_sem.at[dx], twin).start()
    for dx in range(nx):
        theirs = weights.at[:, lax.rem(x - dx + nx, nx) * 2 + 1 - core]
        remote(theirs, theirs, wcs_sem.at[dx], wcr_sem.at[dx], twin).wait_recv()

    def unpack(buf, dy, out):
        wide[...] = buf[pl.ds(dy * nz, nz)].reshape(nz * CAP * tall, LANES).astype(F32)
        here = pl.ds(pl.multiple_of(dy * group, 16), group)
        for part in range(2):
            for c in range(chunks):
                out[part, c, here, :] = wide[pl.ds(part * chunks + c, group, stride=tall), :].astype(BF16)

    step = 256

    def expert(dy, _):
        remote(
            recv.at[pl.ds(dy * nz, nz)], recv.at[pl.ds(dy * nz, nz)], fs_sem, fr_sem.at[dy], twin
        ).wait_recv()
        unpack(recv, dy, xo)
        here = pl.ds(pl.multiple_of(dy * group, 16), group)
        rows_x = jnp.concatenate([xo[0, c, here, :] for c in range(chunks)], axis=1)
        rows_o = jnp.concatenate([xo[1, c, here, :] for c in range(chunks)], axis=1)

        def up(n, _):
            cols = pl.ds(pl.multiple_of(n * step, step), step)
            gate = jnp.dot(rows_x, weights[0, :, :, cols].reshape(width, step), preferred_element_type=F32)
            lift = jnp.dot(rows_x, weights[1, :, :, cols].reshape(width, step), preferred_element_type=F32)
            grad = jnp.dot(rows_o, weights[2, :, :, cols].reshape(width, step), preferred_element_type=F32)
            sigma = jax.nn.sigmoid(gate)
            active = gate * sigma
            slope = sigma * (1.0 + gate * (1.0 - sigma))
            acts[0, here, cols] = (grad * lift * slope).astype(BF16)
            acts[1, here, cols] = (grad * active).astype(BF16)
            acts[2, here, cols] = (active * lift).astype(BF16)
            return 0

        lax.fori_loop(0, hidden_n // step, up, 0)

        def turned(a, m, d):
            w = weights[m, pl.ds(d * 2, 2)].reshape(2 * LANES, hidden_n)
            return lax.dot_general(a, w, (((1,), (1,)), ((), ())), preferred_element_type=F32)

        def down(d, _):
            out = turned(acts[2, here, :], 2, d)
            grad = turned(acts[0, here, :], 0, d) + turned(acts[1, here, :], 1, d)
            for h in range(2):
                cols = slice(h * LANES, (h + 1) * LANES)
                wide[pl.ds(2 * d + h, group, stride=tall), :] = out[:, cols]
                wide[pl.ds(chunks + 2 * d + h, group, stride=tall), :] = grad[:, cols]
            return 0

        lax.fori_loop(0, chunks // 2, down, 0)
        rsend[pl.ds(dy * nz, nz)] = wide[...].astype(BF16).reshape(nz, CAP * tall, LANES)
        scatter(dy, rsend, rrecv, rs_sem, rr_sem, -1)
        return 0

    lax.fori_loop(0, ny, expert, 0)

    def partial(m, shard):
        return lax.dot_general(
            xo[m // 2, shard], acts[m], (((0,), (0,)), ((), ())), preferred_element_type=F32
        )

    def to_twin(i, _):
        dx, m = lax.rem(i // 3 + 1, nx), lax.rem(i, 3)
        csend[i] = partial(m, lax.rem(x + dx, nx) * 2 + 1 - core).astype(BF16)
        remote(csend.at[i], crecv.at[i], gcs_sem.at[i], gcr_sem.at[i], twin).start()
        return 0

    lax.fori_loop(0, 3 * nx, to_twin, 0)

    def along_x(i, _):
        dx, m = lax.rem(i // 3 + 1, nx), lax.rem(i, 3)
        total = partial(m, lax.rem(x + dx, nx) * 2 + core)
        remote(csend.at[i], crecv.at[i], gcs_sem.at[i], gcr_sem.at[i], twin).wait()
        total = total + crecv[i].astype(F32)

        @pl.when(dx > 0)
        def _():
            xsend[i] = total.astype(BF16)
            remote(xsend.at[i], xrecv.at[i], gxs_sem.at[i], gxr_sem.at[i], at_x(dx)).start()

        @pl.when(dx == 0)
        def _():
            acc[m] = total

        return 0

    lax.fori_loop(0, 3 * nx, along_x, 0)

    def returned(dy, _):
        remote(
            rrecv.at[pl.ds(dy * nz, nz)], rrecv.at[pl.ds(dy * nz, nz)], rs_sem, rr_sem.at[dy], twin
        ).wait_recv()
        unpack(rrecv, dy, back)
        return 0

    lax.fori_loop(0, ny - 1, returned, 0)

    early = (ny - 1) * group

    def chosen(start, count):
        lane = lax.broadcasted_iota(jnp.int32, (1, count), 1) + start
        lane_q = fifth(lane)
        wanted = slot_id(lane_q // nz, lane_q & (nz - 1), lane - CAP * lane_q)
        pick = [jnp.where(col_target[k] == wanted, 1.0, 0.0) for k in range(2)]
        return [p.astype(BF16) for p in (pick[0], pick[1], pick[0] + pick[1])]

    def gather(pick, here, c):
        return [jnp.dot(p, back[part, c, here, :], preferred_element_type=F32) for p, part in zip(pick, (0, 0, 1))]

    pick = chosen(0, early)
    for c in range(chunks):
        for k, value in enumerate(gather(pick, slice(0, early), c)):
            picked[k, :, c * LANES:(c + 1) * LANES] = value

    def collect(i, _):
        remote(xsend.at[i], xrecv.at[i], gxs_sem.at[i], gxr_sem.at[i], at_x(lax.rem(i // 3 + 1, nx))).wait()
        m = lax.rem(i, 3)
        acc[m] = acc[m] + xrecv[i].astype(F32)
        return 0

    lax.fori_loop(0, 3 * (nx - 1), collect, 0)
    stores = [pltpu.make_async_copy(acc.at[m], out.at[0], store_sem.at[m]) for m, out in enumerate((og, ou, od))]
    for copy in stores:
        copy.start()

    returned(jnp.int32(ny - 1), 0)
    pick = chosen(early, group)
    sums = [jnp.zeros((rows, 1), F32) for _ in range(2)]
    for c in range(chunks):
        cols = slice(c * LANES, (c + 1) * LANES)
        out = [picked[k, :, cols] + value for k, value in enumerate(gather(pick, slice(early, early + group), c))]
        mixed[:, cols] = (pr[0] * out[0] + pr[1] * out[1]).astype(BF16)
        gtok[:, cols] = out[2].astype(BF16)
        cot_c = cot[:, cols].astype(F32)
        sums = [s + jnp.sum(cot_c * o, axis=1, keepdims=True) for s, o in zip(sums, out)]
    for k in range(2):
        gprob[k:k + 1, :] = jnp.transpose(jnp.broadcast_to(sums[k], (rows, rows)))[0:1, :]

    for copy in stores:
        copy.wait()

    count = ny * nz
    for buf, sem in ((send, fs_sem), (rsend, rs_sem)):
        rest = buf.at[pl.ds(1, count - 1)]
        remote(rest, rest, sem, fr_sem.at[0], twin).wait_send()
    for dx in range(nx):
        remote(mine, mine, wcs_sem.at[dx], wcr_sem.at[dx], twin).wait_send()
        if dx:
            remote(mine, mine, wxs_sem.at[dx], wxr_sem.at[dx], at_x(dx)).wait_send()


def hand_over(*refs):
    count = len(refs) // 3
    sems = refs[-1]
    into = [pltpu.make_async_copy(refs[i], refs[2 * count + i], sems.at[0, i]) for i in range(count)]
    out = [pltpu.make_async_copy(refs[2 * count + i], refs[count + i], sems.at[1, i]) for i in range(count)]
    for copy in into:
        copy.start()
    for first, second in zip(into, out):
        first.wait()
        second.start()
    for copy in out:
        copy.wait()


def per_device(nx, nz_lo, nz_hi, tokens, cotangent, gate_probs, expert_ids, gate_weight, up_weight, down_weight):
    rows, width = tokens.shape
    wide_n = gate_weight.shape[2]
    shard = gate_weight.shape[1]
    experts = nz_lo * nz_hi * NY
    chunks = width // LANES
    tall = 2 * chunks
    slots = experts * CAP
    message = (experts, CAP * tall, LANES)
    vmem = pl.BlockSpec(memory_space=pltpu.VMEM)
    anywhere = pl.BlockSpec(memory_space=pl.ANY)
    dma = pltpu.SemaphoreType.DMA
    grad = jax.ShapeDtypeStruct((1, shard, wide_n), F32)
    pieces = (3 * nx, shard, wide_n)
    shapes = (
        jax.ShapeDtypeStruct((rows, width), BF16),
        jax.ShapeDtypeStruct((rows, width), BF16),
        jax.ShapeDtypeStruct((2, rows), F32),
        grad, grad, grad,
    )
    results = pl.pallas_call(
        functools.partial(kernel, nx, nz_lo, nz_hi, NY),
        out_shape=shapes,
        in_specs=[anywhere] * 2 + [vmem] * 2 + [anywhere] * 3,
        out_specs=(vmem,) * 3 + (anywhere,) * 3,
        scratch_shapes=[
            pltpu.VMEM((rows, width), BF16),
            pltpu.VMEM((rows, width), BF16),
            pltpu.VMEM((3, rows, width), F32),
            pltpu.VMEM((3, 2 * nx, shard, wide_n), BF16),
            pltpu.VMEM(message, BF16),
            pltpu.VMEM(message, BF16),
            pltpu.VMEM(message, BF16),
            pltpu.VMEM(message, BF16),
            pltpu.VMEM((slots // NY * tall, LANES), F32),
            pltpu.VMEM((2, chunks, slots, LANES), BF16),
            pltpu.VMEM((3, slots, wide_n), BF16),
            pltpu.VMEM((2 * rows, width), BF16),
            pltpu.VMEM(pieces, BF16),
            pltpu.VMEM(pieces, BF16),
            pltpu.VMEM(pieces, BF16),
            pltpu.VMEM(pieces, BF16),
            pltpu.VMEM((3, shard, wide_n), F32),
            pltpu.VMEM((2, chunks, slots, LANES), BF16),
            dma((5,)), dma((3,)), dma, dma((NY,)), dma, dma((NY,)),
            dma((nx,)), dma((nx,)), dma((nx,)), dma((nx,)),
            dma((3 * nx,)), dma((3 * nx,)), dma((3 * nx,)), dma((3 * nx,)),
        ],
        compiler_params=pltpu.CompilerParams(
            collective_id=0, has_side_effects=True, vmem_limit_bytes=56 * 2**20
        ),
    )(tokens, cotangent, gate_probs.T, expert_ids.T, gate_weight, up_weight, down_weight)
    mixed, gtok, gprob, *grads = pl.pallas_call(
        hand_over,
        out_shape=shapes,
        in_specs=[anywhere] * 6,
        out_specs=(anywhere,) * 6,
        scratch_shapes=[pltpu.VMEM(a.shape, a.dtype) for a in shapes] + [dma((2, 6))],
    )(*results)
    return (mixed, gtok, gprob.T, *grads)


def solution(mesh):
    tokens = P(("dp", "expouter", "expinner"), None)
    weights = P(("expouter", "expinner"), "dp", None)
    nx = mesh.shape["dp"] // 2
    nz_lo = mesh.shape["expouter"]
    nz_hi = mesh.shape["expinner"] // NY
    return jax.shard_map(
        functools.partial(per_device, nx, nz_lo, nz_hi),
        mesh=mesh,
        in_specs=(tokens,) * 4 + (weights,) * 3,
        out_specs=(tokens,) * 3 + (weights,) * 3,
        check_vma=False,
    )
```

```python
import functools

import jax
import jax.numpy as jnp
from jax import lax
from jax.experimental import pallas as pl
from jax.experimental.pallas import tpu as pltpu
from jax.sharding import PartitionSpec as P

MESH = pl.DeviceIdType.MESH
F32 = jnp.float32
BF16 = jnp.bfloat16
LANES = 128
NY = 4
CAP = 5


def fifth(v):
    return (v * 52429) >> 18


def kernel(
    nx, nz_lo, nz_hi, ny,
    tok_in, cot_in, probs, ids, wg, wu, wd,
    mixed, gtok, gprob, og, ou, od,
    tok, cot, picked, weights, send, recv, rsend, rrecv, wide, xo, acts, scaled,
    csend, crecv, xsend, xrecv, acc, back,
    load_sem, store_sem, fs_sem, fr_sem, rs_sem, rr_sem,
    wxs_sem, wxr_sem, wcs_sem, wcr_sem,
    gcs_sem, gcr_sem, gxs_sem, gxr_sem,
):
    nz = nz_lo * nz_hi
    rows, width = tok.shape
    chunks = width // LANES
    tall = 2 * chunks
    group = nz * CAP
    hidden_n = wg.shape[2]
    me = lax.axis_index("dp")
    x, core = me // 2, me % 2
    inner = lax.axis_index("expinner")
    y = inner % ny
    z = (inner // ny) * nz_lo + lax.axis_index("expouter")

    def at_yz(dy, dz):
        tz = lax.rem(z + dz + nz, nz)
        ty = lax.rem(y + dy + ny, ny)
        return {"expouter": lax.rem(tz, nz_lo), "expinner": (tz // nz_lo) * ny + ty}

    def at_x(dx):
        return {"dp": lax.rem(x + dx, nx) * 2 + core}

    twin = {"dp": x * 2 + 1 - core}

    def remote(src, dst, ss, rs, device):
        return pltpu.make_async_remote_copy(
            src_ref=src, dst_ref=dst, send_sem=ss, recv_sem=rs,
            device_id=device, device_id_type=MESH,
        )

    loads = [
        pltpu.make_async_copy(a, b, load_sem.at[i])
        for i, (a, b) in enumerate(
            [(tok_in, tok), (cot_in, cot)]
            + [(w.at[0], weights.at[m, me]) for m, w in enumerate((wg, wu, wd))]
        )
    ]
    barrier = pltpu.get_barrier_semaphore()

    for dz in sorted(range(nz), key=lambda d: -min(d, nz - d)):
        for dy in range(ny):
            if dy or dz:
                tz = (z + dz) & (nz - 1)
                ty = (y + dy) & (ny - 1)
                there = {"expouter": tz & (nz_lo - 1), "expinner": (tz // nz_lo) * ny + ty}
                pl.semaphore_signal(barrier, inc=1, device_id=there, device_id_type=MESH)
    for dx in range(1, nx):
        pl.semaphore_signal(barrier, inc=1, device_id=at_x(dx), device_id_type=MESH)
    pl.semaphore_signal(barrier, inc=1, device_id=twin, device_id_type=MESH)
    for copy in loads:
        copy.start()

    idf = ids[...].astype(F32)
    over_id = [jnp.broadcast_to(idf[k:k + 1, :], (rows, rows)) for k in range(2)]
    down_id = [jnp.transpose(b) for b in over_id]
    first = lax.broadcasted_iota(jnp.int32, (rows, rows), 0)
    second = lax.broadcasted_iota(jnp.int32, (rows, rows), 1)
    col_target, row_target = [], []
    for k in range(2):
        hits = sum(jnp.where((down_id[k] == over_id[j]) & (second < first), 1.0, 0.0) for j in range(2))
        col_target.append(down_id[k][:, 0:1] * CAP + jnp.sum(hits, axis=1, keepdims=True))
        hits = sum(jnp.where((down_id[j] == over_id[k]) & (first < second), 1.0, 0.0) for j in range(2))
        row_target.append(idf[k:k + 1, :] * CAP + jnp.sum(hits, axis=0, keepdims=True))
    pr = [jnp.transpose(jnp.broadcast_to(probs[k:k + 1, :], (rows, rows)))[:, 0:1] for k in range(2)]
    for copy in loads[:2]:
        copy.wait()
    for k in range(2):
        scaled[k * rows:(k + 1) * rows, :] = (pr[k] * cot[...].astype(F32)).astype(BF16)

    def slot_id(dy, q, slot):
        tz = (z + q) & (nz - 1)
        ty = (y + dy) & (ny - 1)
        expert = (tz & (nz_lo - 1)) * (nz_hi * ny) + (tz // nz_lo) * ny + ty
        return (expert * CAP + slot).astype(F32)

    line = lax.broadcasted_iota(jnp.int32, (group, 1), 0)
    line_dz = fifth(line)
    line_slot = line - CAP * line_dz

    def pack(dy):
        wanted = slot_id(dy, line_dz, line_slot)
        sel = [jnp.where(wanted == row_target[k], 1.0, 0.0) for k in range(2)]
        both = (sel[0] + sel[1]).astype(BF16)
        each = jnp.concatenate(sel, axis=1).astype(BF16)
        rows_x = jnp.dot(both, tok[...], preferred_element_type=F32)
        rows_o = jnp.dot(each, scaled[...], preferred_element_type=F32)
        for c in range(chunks):
            cols = slice(c * LANES, (c + 1) * LANES)
            wide[pl.ds(c, group, stride=tall), :] = rows_x[:, cols]
            wide[pl.ds(chunks + c, group, stride=tall), :] = rows_o[:, cols]
        send[pl.ds(dy * nz, nz)] = wide[...].astype(BF16).reshape(nz, CAP * tall, LANES)

    def scatter(dy, src, dst, ss, rs, sign):
        def one(n, _):
            j = nz - 1 - n
            dz = jnp.where(lax.rem(j, 2) == 1, (j + 1) // 2, lax.rem(nz - j // 2, nz))
            if sign < 0:
                dz = lax.rem(z - n + nz, nz)
            i = dy * nz + dz

            @pl.when(i > 0)
            def _():
                remote(src.at[i], dst.at[i], ss, rs.at[dy], at_yz(sign * dy, sign * dz)).start()

            return 0

        lax.fori_loop(0, nz, one, 0)

        @pl.when(dy == 0)
        def _():
            pltpu.make_async_copy(src.at[0], dst.at[0], rs.at[0]).start()

    pack(jnp.int32(0))
    for copy in loads[2:]:
        copy.wait()
    pl.semaphore_wait(barrier, ny * nz - 1 + nx - 1 + 1)
    scatter(jnp.int32(0), send, recv, fs_sem, fr_sem, 1)

    mine = weights.at[:, me]
    remote(mine, mine, wcs_sem.at[0], wcr_sem.at[0], twin).start()
    for dx in range(1, nx):
        remote(mine, mine, wxs_sem.at[dx], wxr_sem.at[dx], at_x(dx)).start()

    def pack_and_send(dy, _):
        pack(dy)
        scatter(dy, send, recv, fs_sem, fr_sem, 1)
        return 0

    lax.fori_loop(1, ny, pack_and_send, 0)

    for dx in range(1, nx):
        theirs = weights.at[:, lax.rem(x - dx + nx, nx) * 2 + core]
        remote(theirs, theirs, wxs_sem.at[dx], wxr_sem.at[dx], at_x(dx)).wait_recv()
        remote(theirs, theirs, wcs_sem.at[dx], wcr_sem.at[dx], twin).start()
    for dx in range(nx):
        theirs = weights.at[:, lax.rem(x - dx + nx, nx) * 2 + 1 - core]
        remote(theirs, theirs, wcs_sem.at[dx], wcr_sem.at[dx], twin).wait_recv()

    def unpack(buf, dy, out):
        wide[...] = buf[pl.ds(dy * nz, nz)].reshape(nz * CAP * tall, LANES).astype(F32)
        here = pl.ds(pl.multiple_of(dy * group, 16), group)
        for part in range(2):
            for c in range(chunks):
                out[part, c, here, :] = wide[pl.ds(part * chunks + c, group, stride=tall), :].astype(BF16)

    step = 256

    def expert(dy, _):
        remote(
            recv.at[pl.ds(dy * nz, nz)], recv.at[pl.ds(dy * nz, nz)], fs_sem, fr_sem.at[dy], twin
        ).wait_recv()
        unpack(recv, dy, xo)
        here = pl.ds(pl.multiple_of(dy * group, 16), group)
        rows_x = jnp.concatenate([xo[0, c, here, :] for c in range(chunks)], axis=1)
        rows_o = jnp.concatenate([xo[1, c, here, :] for c in range(chunks)], axis=1)

        def up(n, _):
            cols = pl.ds(pl.multiple_of(n * step, step), step)
            gate = jnp.dot(rows_x, weights[0, :, :, cols].reshape(width, step), preferred_element_type=F32)
            lift = jnp.dot(rows_x, weights[1, :, :, cols].reshape(width, step), preferred_element_type=F32)
            grad = jnp.dot(rows_o, weights[2, :, :, cols].reshape(width, step), preferred_element_type=F32)
            sigma = jax.nn.sigmoid(gate)
            active = gate * sigma
            slope = sigma * (1.0 + gate * (1.0 - sigma))
            acts[0, here, cols] = (grad * lift * slope).astype(BF16)
            acts[1, here, cols] = (grad * active).astype(BF16)
            acts[2, here, cols] = (active * lift).astype(BF16)
            return 0

        lax.fori_loop(0, hidden_n // step, up, 0)

        def turned(a, m, d):
            w = weights[m, pl.ds(d * 2, 2)].reshape(2 * LANES, hidden_n)
            return lax.dot_general(a, w, (((1,), (1,)), ((), ())), preferred_element_type=F32)

        def down(d, _):
            out = turned(acts[2, here, :], 2, d)
            grad = turned(acts[0, here, :], 0, d) + turned(acts[1, here, :], 1, d)
            for h in range(2):
                cols = slice(h * LANES, (h + 1) * LANES)
                wide[pl.ds(2 * d + h, group, stride=tall), :] = out[:, cols]
                wide[pl.ds(chunks + 2 * d + h, group, stride=tall), :] = grad[:, cols]
            return 0

        lax.fori_loop(0, chunks // 2, down, 0)
        rsend[pl.ds(dy * nz, nz)] = wide[...].astype(BF16).reshape(nz, CAP * tall, LANES)
        scatter(dy, rsend, rrecv, rs_sem, rr_sem, -1)
        return 0

    lax.fori_loop(0, ny, expert, 0)

    def partial(m, shard):
        return lax.dot_general(
            xo[m // 2, shard], acts[m], (((0,), (0,)), ((), ())), preferred_element_type=F32
        )

    def to_twin(i, _):
        dx, m = lax.rem(i // 3 + 1, nx), lax.rem(i, 3)
        csend[i] = partial(m, lax.rem(x + dx, nx) * 2 + 1 - core).astype(BF16)
        remote(csend.at[i], crecv.at[i], gcs_sem.at[i], gcr_sem.at[i], twin).start()
        return 0

    lax.fori_loop(0, 3 * nx, to_twin, 0)

    def along_x(i, _):
        dx, m = lax.rem(i // 3 + 1, nx), lax.rem(i, 3)
        total = partial(m, lax.rem(x + dx, nx) * 2 + core)
        remote(csend.at[i], crecv.at[i], gcs_sem.at[i], gcr_sem.at[i], twin).wait()
        total = total + crecv[i].astype(F32)

        @pl.when(dx > 0)
        def _():
            xsend[i] = total.astype(BF16)
            remote(xsend.at[i], xrecv.at[i], gxs_sem.at[i], gxr_sem.at[i], at_x(dx)).start()

        @pl.when(dx == 0)
        def _():
            acc[m] = total

        return 0

    lax.fori_loop(0, 3 * nx, along_x, 0)

    def returned(dy, _):
        remote(
            rrecv.at[pl.ds(dy * nz, nz)], rrecv.at[pl.ds(dy * nz, nz)], rs_sem, rr_sem.at[dy], twin
        ).wait_recv()
        unpack(rrecv, dy, back)
        return 0

    lax.fori_loop(0, ny - 1, returned, 0)

    early = (ny - 1) * group

    def chosen(start, count):
        lane = lax.broadcasted_iota(jnp.int32, (1, count), 1) + start
        lane_q = fifth(lane)
        wanted = slot_id(lane_q // nz, lane_q & (nz - 1), lane - CAP * lane_q)
        pick = [jnp.where(col_target[k] == wanted, 1.0, 0.0) for k in range(2)]
        return [p.astype(BF16) for p in (pick[0], pick[1], pick[0] + pick[1])]

    def gather(pick, here, c):
        return [jnp.dot(p, back[part, c, here, :], preferred_element_type=F32) for p, part in zip(pick, (0, 0, 1))]

    pick = chosen(0, early)
    for c in range(chunks):
        for k, value in enumerate(gather(pick, slice(0, early), c)):
            picked[k, :, c * LANES:(c + 1) * LANES] = value

    def collect(i, _):
        remote(xsend.at[i], xrecv.at[i], gxs_sem.at[i], gxr_sem.at[i], at_x(lax.rem(i // 3 + 1, nx))).wait()
        m = lax.rem(i, 3)
        acc[m] = acc[m] + xrecv[i].astype(F32)
        return 0

    lax.fori_loop(0, 3 * (nx - 1), collect, 0)
    stores = [pltpu.make_async_copy(acc.at[m], out.at[0], store_sem.at[m]) for m, out in enumerate((og, ou, od))]
    for copy in stores:
        copy.start()

    last = pl.ds((ny - 1) * nz, nz)
    remote(rrecv.at[last], rrecv.at[last], rs_sem, rr_sem.at[ny - 1], twin).wait_recv()
    wide[...] = rrecv[last].reshape(nz * CAP * tall, LANES).astype(F32)
    pick = chosen(early, group)
    stacked = jnp.concatenate(pick[:2], axis=0)
    sums = [jnp.zeros((rows, 1), F32) for _ in range(2)]
    for c in range(chunks):
        cols = slice(c * LANES, (c + 1) * LANES)
        out_rows = wide[pl.ds(c, group, stride=tall), :].astype(BF16)
        grad_rows = wide[pl.ds(chunks + c, group, stride=tall), :].astype(BF16)
        pair = jnp.dot(stacked, out_rows, preferred_element_type=F32)
        out = [picked[k, :, cols] + pair[k * rows:(k + 1) * rows] for k in range(2)]
        out.append(picked[2, :, cols] + jnp.dot(pick[2], grad_rows, preferred_element_type=F32))
        mixed[:, cols] = (pr[0] * out[0] + pr[1] * out[1]).astype(BF16)
        gtok[:, cols] = out[2].astype(BF16)
        cot_c = cot[:, cols].astype(F32)
        sums = [s + jnp.sum(cot_c * o, axis=1, keepdims=True) for s, o in zip(sums, out)]
    for k in range(2):
        gprob[k:k + 1, :] = jnp.transpose(jnp.broadcast_to(sums[k], (rows, rows)))[0:1, :]

    for copy in stores:
        copy.wait()

    count = ny * nz
    for buf, sem in ((send, fs_sem), (rsend, rs_sem)):
        rest = buf.at[pl.ds(1, count - 1)]
        remote(rest, rest, sem, fr_sem.at[0], twin).wait_send()
    for dx in range(nx):
        remote(mine, mine, wcs_sem.at[dx], wcr_sem.at[dx], twin).wait_send()
        if dx:
            remote(mine, mine, wxs_sem.at[dx], wxr_sem.at[dx], at_x(dx)).wait_send()


def hand_over(*refs):
    count = len(refs) // 3
    sems = refs[-1]
    into = [pltpu.make_async_copy(refs[i], refs[2 * count + i], sems.at[0, i]) for i in range(count)]
    out = [pltpu.make_async_copy(refs[2 * count + i], refs[count + i], sems.at[1, i]) for i in range(count)]
    for copy in into:
        copy.start()
    for first, second in zip(into, out):
        first.wait()
        second.start()
    for copy in out:
        copy.wait()


def per_device(nx, nz_lo, nz_hi, tokens, cotangent, gate_probs, expert_ids, gate_weight, up_weight, down_weight):
    rows, width = tokens.shape
    wide_n = gate_weight.shape[2]
    shard = gate_weight.shape[1]
    experts = nz_lo * nz_hi * NY
    chunks = width // LANES
    tall = 2 * chunks
    slots = experts * CAP
    message = (experts, CAP * tall, LANES)
    vmem = pl.BlockSpec(memory_space=pltpu.VMEM)
    anywhere = pl.BlockSpec(memory_space=pl.ANY)
    dma = pltpu.SemaphoreType.DMA
    grad = jax.ShapeDtypeStruct((1, shard, wide_n), F32)
    pieces = (3 * nx, shard, wide_n)
    shapes = (
        jax.ShapeDtypeStruct((rows, width), BF16),
        jax.ShapeDtypeStruct((rows, width), BF16),
        jax.ShapeDtypeStruct((2, rows), F32),
        grad, grad, grad,
    )
    results = pl.pallas_call(
        functools.partial(kernel, nx, nz_lo, nz_hi, NY),
        out_shape=shapes,
        in_specs=[anywhere] * 2 + [vmem] * 2 + [anywhere] * 3,
        out_specs=(vmem,) * 3 + (anywhere,) * 3,
        scratch_shapes=[
            pltpu.VMEM((rows, width), BF16),
            pltpu.VMEM((rows, width), BF16),
            pltpu.VMEM((3, rows, width), F32),
            pltpu.VMEM((3, 2 * nx, shard, wide_n), BF16),
            pltpu.VMEM(message, BF16),
            pltpu.VMEM(message, BF16),
            pltpu.VMEM(message, BF16),
            pltpu.VMEM(message, BF16),
            pltpu.VMEM((slots // NY * tall, LANES), F32),
            pltpu.VMEM((2, chunks, slots, LANES), BF16),
            pltpu.VMEM((3, slots, wide_n), BF16),
            pltpu.VMEM((2 * rows, width), BF16),
            pltpu.VMEM(pieces, BF16),
            pltpu.VMEM(pieces, BF16),
            pltpu.VMEM(pieces, BF16),
            pltpu.VMEM(pieces, BF16),
            pltpu.VMEM((3, shard, wide_n), F32),
            pltpu.VMEM((2, chunks, slots, LANES), BF16),
            dma((5,)), dma((3,)), dma, dma((NY,)), dma, dma((NY,)),
            dma((nx,)), dma((nx,)), dma((nx,)), dma((nx,)),
            dma((3 * nx,)), dma((3 * nx,)), dma((3 * nx,)), dma((3 * nx,)),
        ],
        compiler_params=pltpu.CompilerParams(
            collective_id=0, has_side_effects=True, vmem_limit_bytes=56 * 2**20
        ),
    )(tokens, cotangent, gate_probs.T, expert_ids.T, gate_weight, up_weight, down_weight)
    mixed, gtok, gprob, *grads = pl.pallas_call(
        hand_over,
        out_shape=shapes,
        in_specs=[anywhere] * 6,
        out_specs=(anywhere,) * 6,
        scratch_shapes=[pltpu.VMEM(a.shape, a.dtype) for a in shapes] + [dma((2, 6))],
    )(*results)
    return (mixed, gtok, gprob.T, *grads)


def solution(mesh):
    tokens = P(("dp", "expouter", "expinner"), None)
    weights = P(("expouter", "expinner"), "dp", None)
    nx = mesh.shape["dp"] // 2
    nz_lo = mesh.shape["expouter"]
    nz_hi = mesh.shape["expinner"] // NY
    return jax.shard_map(
        functools.partial(per_device, nx, nz_lo, nz_hi),
        mesh=mesh,
        in_specs=(tokens,) * 4 + (weights,) * 3,
        out_specs=(tokens,) * 3 + (weights,) * 3,
        check_vma=False,
    )
```
